32 devices in a mesh: fsdp: 8 (over z, x), dp: 4 (over y, core).
Axes of the slice: x: 2, y: 2, z: 4, core: 2. Of those that a mesh axis runs over, the one named last changes fastest.
Arguments:
- tokens: bfloat16 [192, 197, 768], P(('fsdp', 'dp')), may hold values from -6 to 6
- w_qkv: bfloat16 [768, 2304], P(('fsdp', 'dp')), may hold values from -0.21875 to 0.21875
- w_out: bfloat16 [768, 768], P(('fsdp', 'dp')), may hold values from -1.25 to 1.25
- w_up: bfloat16 [768, 3072], P(('fsdp', 'dp')), may hold values from -0.21875 to 0.21875
- w_down: bfloat16 [3072, 768], P(('fsdp', 'dp')), may hold values from -0.109375 to 0.109375
- norm1_scale: bfloat16 [768], P(('fsdp', 'dp')), may hold values from 0.25 to 1.75
- norm1_offset: bfloat16 [768], P(('fsdp', 'dp')), may hold values from -4 to 4
- qv_bias: bfloat16 [1536], P(('fsdp', 'dp')), may hold values from -6 to 6
- out_bias: bfloat16 [768], P(('fsdp', 'dp')), may hold values from -4 to 4
- norm2_scale: bfloat16 [768], P(('fsdp', 'dp')), may hold values from 0.25 to 1.75
- norm2_offset: bfloat16 [768], P(('fsdp', 'dp')), may hold values from -4 to 4
- up_bias: bfloat16 [3072], P(('fsdp', 'dp')), may hold values from -6 to 6
- down_bias: bfloat16 [768], P(('fsdp', 'dp')), may hold values from -4 to 4
- cotangent: bfloat16 [192, 197, 768], P(('fsdp', 'dp')), may hold values from -6 to 6
- counts: int32 [32], P(('fsdp', 'dp')), may hold values from 1 to 6, 128 in all
Outputs:
- out_tokens: bfloat16 [192, 197, 768], P(('fsdp', 'dp'))
- grad_tokens: float32 [192, 197, 768], P(('fsdp', 'dp'))
- grad_w_qkv: float32 [768, 2304], P(('fsdp', 'dp'))
- grad_w_out: float32 [768, 768], P(('fsdp', 'dp'))
- grad_w_up: float32 [768, 3072], P(('fsdp', 'dp'))
- grad_w_down: float32 [3072, 768], P(('fsdp', 'dp'))
- grad_norm1_scale: float32 [768], P(('fsdp', 'dp'))
- grad_norm1_offset: float32 [768], P(('fsdp', 'dp'))
- grad_qv_bias: float32 [1536], P(('fsdp', 'dp'))
- grad_out_bias: float32 [768], P(('fsdp', 'dp'))
- grad_norm2_scale: float32 [768], P(('fsdp', 'dp'))
- grad_norm2_offset: float32 [768], P(('fsdp', 'dp'))
- grad_up_bias: float32 [3072], P(('fsdp', 'dp'))
- grad_down_bias: float32 [768], P(('fsdp', 'dp'))
The draws below stay inside these ranges and needn't reach their ends.
Inputs may be any that keep to these rules, and one draw needn't show every extreme that they name: counts[i] is the number of images of the i-th device along fsdp+dp, which fill the first of its 6 slots; the entries sum to 128.
All inputs are finite; a program needn't handle non-finite values.
Results may differ from the reference program's by a relative error of at most 0.011.
Values may be sent and summed in bfloat16 or wider, within the bound.
No kernel may reach another device: no remote copies, remote signals or barrier semaphores. Data moves between devices by JAX's collectives and lax.ppermute only.
A program may use at most 192 MiB of HBM per device.

```python
import math
import jax
import jax.numpy as jnp
import numpy as np
from jax import lax

D = 768
HEADS = 12
FF = 3072
SEQ = 197
CAP = 6
SLOTS = 192
IMAGES = 128
DEVICES = 32


def strengthened(array, key, source, target, blocks, factor):
    def block_of(axis_at):
        return (jnp.arange(array.shape[axis_at]) // (array.shape[axis_at] // blocks)).reshape((-1,) + (1,) * (array.ndim - 1 - axis_at))

    first = jax.random.permutation(key, blocks)[block_of(target)]
    far = (block_of(target) + blocks // 2) % blocks
    return jnp.where((block_of(source) == first) | (block_of(source) == far), factor * array, array)


def block_levels(stream_key, dims, cuts, least, top_value):
    loudness = 1.0
    for dim, parts in cuts:
        draws = jax.random.uniform(jax.random.fold_in(jax.random.fold_in(stream_key, 6), dim), (parts,), jnp.float32, least / len(cuts), top_value / len(cuts))
        loudness = loudness * jnp.repeat(jnp.exp(draws), dims[dim] // parts).reshape((-1,) + (1,) * (len(dims) - 1 - dim))
    return loudness


def length_profile(number_of, total, limit, slope):
    loads = [(1 << 20) // math.isqrt(grade ** slope) + 1 for grade in range(2, number_of + 1)]
    rest, given = total - limit - (number_of - 1), [1] * (number_of - 1)
    while rest > 0:
        candidates = [i for i in range(number_of - 1) if given[i] < limit]
        mass, budget = sum([loads[i] for i in candidates]), rest
        for i in candidates:
            more = min(limit - given[i], max(1, budget * loads[i] // mass), rest)
            given[i] = given[i] + more
            rest = rest - more
    return np.array([limit] + given)


def ragged(stream_key, count, total, limit, slope):
    if count == 2:
        one = jax.random.randint(stream_key, (), max(1, total - limit), min(limit, total - 1) + 1)
        return jnp.stack([one, total - one])
    sizes = jnp.asarray(length_profile(count, total, limit, slope), jnp.int32)
    pairs = (count - 1) // 2
    source_of, receiver = sizes[1:1 + 2 * pairs:2], sizes[2:2 + 2 * pairs:2]
    margin = jnp.minimum(source_of - 1, limit - receiver)
    moved = jax.random.randint(jax.random.fold_in(stream_key, 1), (pairs,), 0, 1 << 20) % (margin + 1)
    sizes = sizes.at[1:1 + 2 * pairs:2].set(source_of - moved).at[2:2 + 2 * pairs:2].set(receiver + moved)
    return sizes[jax.random.permutation(jax.random.fold_in(stream_key, 2), count)]


def bell_draw(own_key, extent, scale, limit, cuts=(), kind=jnp.bfloat16):
    values = jax.random.normal(own_key, extent, jnp.float32) * scale
    if len(cuts) > 0:
        values = block_levels(own_key, extent, cuts, -0.22, 0.18) * values
    return jnp.clip(values, min=-limit, max=limit).astype(kind)


def noise_with(key, extent, scale, reach, cuts, heavy, kind=jnp.bfloat16):
    values = scale * jax.random.normal(key, extent, jnp.float32)
    if cuts:
        values = values * block_levels(key, extent, cuts, -0.22, 0.18)
    return jnp.clip(strengthened(values, jax.random.fold_in(key, 3), *heavy), -reach, reach).astype(kind)


def setup_inputs(seed: int = 0) -> dict:
    seeds = jax.random.split(jax.random.key(seed), 16)
    tokens = bell_draw(seeds[0], (SLOTS, SEQ, D), 1.0, 6.0, ((0, 32),))
    w_qkv = bell_draw(seeds[1], (D, 3 * D), D ** -0.5, 0.21875, ((0, 32),))
    w_out = bell_draw(seeds[2], (D, D), (D // 32) ** -0.5, 1.25, ((0, 32),))
    w_up = bell_draw(seeds[3], (D, FF), D ** -0.5, 0.21875, ((0, 32),))
    w_down = bell_draw(seeds[4], (FF, D), FF ** -0.5, 0.109375, ((0, 32),))
    norm1_scale = jnp.clip(1.0 + 0.15 * jax.random.normal(seeds[5], (D,), jnp.float32), 0.25, 1.75).astype(jnp.bfloat16)
    norm1_offset = bell_draw(seeds[6], (D,), 0.3, 4.0, ((0, 32),))
    qv_bias = bell_draw(seeds[7], (2 * D,), 0.5, 6.0, ((0, 32),))
    out_bias = bell_draw(seeds[8], (D,), 0.3, 4.0, ((0, 32),))
    norm2_scale = jnp.clip(1.0 + 0.15 * jax.random.normal(seeds[9], (D,), jnp.float32), 0.25, 1.75).astype(jnp.bfloat16)
    norm2_offset = bell_draw(seeds[10], (D,), 0.3, 4.0, ((0, 32),))
    up_bias = bell_draw(seeds[11], (FF,), 0.5, 6.0, ((0, 32),))
    down_bias = bell_draw(seeds[12], (D,), 0.3, 4.0, ((0, 32),))
    cotangent = noise_with(seeds[13], (SLOTS, SEQ, D), 1.0, 6.0, ((0, 32),), (0, 2, 32, 2.75))
    counts = ragged(seeds[14], DEVICES, IMAGES, CAP, 2).astype(jnp.int32)
    return {"tokens": tokens, "w_qkv": w_qkv, "w_out": w_out, "w_up": w_up, "w_down": w_down, "norm1_scale": norm1_scale, "norm1_offset": norm1_offset, "qv_bias": qv_bias, "out_bias": out_bias, "norm2_scale": norm2_scale, "norm2_offset": norm2_offset, "up_bias": up_bias, "down_bias": down_bias, "cotangent": cotangent, "counts": counts}


EPSILON = 1e-06
HIGHEST = lax.Precision.HIGHEST

@jax.custom_vjp
def low(v):
    return lax.optimization_barrier(v.astype(jnp.bfloat16)).astype(jnp.float32)

@jax.custom_vjp
def low_back(v):
    return v

def low_keep(v):
    return (low(v), None)

def low_pass(kept, grad):
    return (grad,)

def back_keep(v):
    return (v, None)

def back_low(kept, grad):
    return (low(grad),)
low.defvjp(low_keep, low_pass)
low_back.defvjp(back_keep, back_low)

def norm_rows(values, scale_vec, offset):
    center = values - lax.optimization_barrier(jnp.mean(values, axis=-1, keepdims=True))
    spread = lax.optimization_barrier(jnp.mean(center * center, axis=-1, keepdims=True))
    return center * lax.rsqrt(spread + EPSILON) * scale_vec + offset

def block_forward(params, inputs, live_slots):
    w_qkv, w_out, w_up, w_down, scale_one, offset_one, qv_bias, out_bias, scale_two, offset_two, up_bias, down_bias = params
    model_width = inputs.shape[-1]
    head_size = model_width // HEADS
    normed = low(norm_rows(inputs, scale_one, offset_one))
    bias_full = jnp.concatenate([qv_bias[:model_width], jnp.zeros((model_width,), qv_bias.dtype), qv_bias[model_width:]])
    projected = jnp.einsum('bsd,de->bse', normed, w_qkv, precision=HIGHEST) + bias_full
    projected = low(low_back(projected))
    split_shape = inputs.shape[:2] + (HEADS, head_size)
    queries = projected[..., :model_width].reshape(split_shape)
    key_rows = projected[..., model_width:2 * model_width].reshape(split_shape)
    value_rows = projected[..., 2 * model_width:].reshape(split_shape)
    raw_scores = low_back(jnp.einsum('bqhd,bkhd->bhqk', queries, key_rows, precision=HIGHEST)) * head_size ** (-0.5)
    probs_low = low(jax.nn.softmax(raw_scores, axis=-1))
    head_out = jnp.einsum('bhqk,bkhd->bqhd', probs_low, value_rows, precision=HIGHEST)
    head_out = low(low_back(head_out)).reshape(inputs.shape)
    branch = low_back(jnp.einsum('bsd,de->bse', head_out, w_out, precision=HIGHEST) + out_bias)
    middle = inputs + branch
    normed_two = low(norm_rows(middle, scale_two, offset_two))
    hidden = low_back(jnp.einsum('bsd,df->bsf', normed_two, w_up, precision=HIGHEST) + up_bias)
    active = low(jax.nn.gelu(hidden, approximate=False))
    branch_two = low_back(jnp.einsum('bsf,fd->bsd', active, w_down, precision=HIGHEST) + down_bias)
    return (middle + branch_two) * live_slots[:, None, None]

def reference(tokens, w_qkv, w_out, w_up, w_down, norm1_scale, norm1_offset, qv_bias, out_bias, norm2_scale, norm2_offset, up_bias, down_bias, cotangent, counts):
    params = (w_qkv.astype(jnp.float32), w_out.astype(jnp.float32), w_up.astype(jnp.float32), w_down.astype(jnp.float32), norm1_scale.astype(jnp.float32), norm1_offset.astype(jnp.float32), qv_bias.astype(jnp.float32), out_bias.astype(jnp.float32), norm2_scale.astype(jnp.float32), norm2_offset.astype(jnp.float32), up_bias.astype(jnp.float32), down_bias.astype(jnp.float32))
    inputs = tokens.astype(jnp.float32)
    slot_count = tokens.shape[0]
    holders = counts.shape[0]
    slot_place = jnp.arange(slot_count).astype(jnp.int32) % CAP
    live_all = (slot_place < jnp.repeat(counts, CAP, total_repeat_length=slot_count)).astype(jnp.float32)
    live_grouped = live_all.reshape(holders, CAP)
    block_step = jax.checkpoint(block_forward)

    def whole_layer(params, inputs):
        grouped = inputs.reshape((holders, CAP) + inputs.shape[1:])

        def advance(carry, item_pair):
            return (carry, block_step(params, item_pair[0], item_pair[1]))
        unused, outputs = lax.scan(advance, jnp.zeros((), jnp.float32), (grouped, live_grouped))
        return outputs.reshape(inputs.shape)
    result, pullback = jax.vjp(whole_layer, params, inputs)
    grad_params, grad_inputs = pullback(cotangent.astype(jnp.float32))
    return (result.astype(jnp.bfloat16), grad_inputs, grad_params[0], grad_params[1], grad_params[2], grad_params[3], grad_params[4], grad_params[5], grad_params[6], grad_params[7], grad_params[8], grad_params[9], grad_params[10], grad_params[11])
```

```python
import functools
import math

import jax
import jax.numpy as jnp
from jax import lax
from jax.experimental import pallas as pl
from jax.experimental.pallas import tpu as pltpu
from jax.sharding import PartitionSpec as P

HEADS = 12
EPSILON = 1e-06
AXES = ("fsdp", "dp")
LOW = jnp.bfloat16
WIDE = jnp.float32
NN = (((1,), (0,)), ((), ()))
NT = (((1,), (1,)), ((), ()))
TN = (((0,), (0,)), ((), ()))


def dot(a, b, dims=NN):
    return lax.dot_general(a, b, dims, preferred_element_type=WIDE)


def attend(seq_len, factor, proj_ref, out_ref):
    rows, model_width = out_ref.shape[1:]
    lane = lax.broadcasted_iota(jnp.int32, (1, 128), 1)
    key_at = lax.broadcasted_iota(jnp.int32, (1, rows), 1)
    ones = jnp.ones((rows, 128), jnp.bfloat16)
    zero = jnp.zeros((), jnp.bfloat16)
    for pair in range(model_width // 128):
        at = pair * 128
        queries = proj_ref[0, :, at : at + 128]
        keys = proj_ref[0, :, model_width + at : model_width + at + 128]
        values = proj_ref[0, :, 2 * model_width + at : 2 * model_width + at + 128]
        wide = jnp.concatenate([values, ones], axis=1)
        halves = []
        for half in range(2):
            mine = (lane < 64) if half == 0 else (lane >= 64)
            scores = dot(jnp.where(mine, queries, zero), keys, NT)
            scores = jnp.where(key_at < seq_len, scores, -jnp.inf)
            top = jnp.max(scores, axis=1, keepdims=True)
            expo = jnp.exp((scores - top) * factor).astype(jnp.bfloat16)
            both = dot(expo, wide, NN)
            halves.append(both[:, :128] / both[:, 128:])
        out_ref[0, :, at : at + 128] = jnp.where(lane < 64, halves[0], halves[1]).astype(jnp.bfloat16)


def attend_back(seq_len, factor, proj_ref, back_ref, out_ref):
    rows, model_width = back_ref.shape[1:]
    lane = lax.broadcasted_iota(jnp.int32, (1, 128), 1)
    key_at = lax.broadcasted_iota(jnp.int32, (rows, 1), 0)
    zero = jnp.zeros((), jnp.bfloat16)
    for pair in range(model_width // 128):
        at = pair * 128
        queries = proj_ref[0, :, at : at + 128]
        keys = proj_ref[0, :, model_width + at : model_width + at + 128]
        values = proj_ref[0, :, 2 * model_width + at : 2 * model_width + at + 128]
        back = back_ref[0, :, at : at + 128]
        parts = []
        for half in range(2):
            mine = (lane < 64) if half == 0 else (lane >= 64)
            queries_one = jnp.where(mine, queries, zero)
            back_one = jnp.where(mine, back, zero)
            scores = dot(keys, queries_one, NT)
            scores = jnp.where(key_at < seq_len, scores, -jnp.inf)
            top = jnp.max(scores, axis=0, keepdims=True)
            expo = jnp.exp((scores - top) * factor)
            probs = expo * (1.0 / jnp.sum(expo, axis=0, keepdims=True))
            back_probs = dot(values, back_one, NT)
            weighted = probs * back_probs
            row_dot = jnp.sum(weighted, axis=0, keepdims=True)
            scaled = ((weighted - probs * row_dot) * factor).astype(jnp.bfloat16)
            parts.append(
                (
                    dot(scaled, keys, TN),
                    dot(scaled, queries_one, NN),
                    dot(probs.astype(jnp.bfloat16), back_one, NN),
                )
            )
        first, second = parts
        out_ref[0, :, at : at + 128] = jnp.where(lane < 64, first[0], second[0]).astype(jnp.bfloat16)
        out_ref[0, :, model_width + at : model_width + at + 128] = (first[1] + second[1]).astype(jnp.bfloat16)
        out_ref[0, :, 2 * model_width + at : 2 * model_width + at + 128] = (first[2] + second[2]).astype(jnp.bfloat16)


def whole(shape):
    return pl.BlockSpec((1,) + shape, lambda i: (i, 0, 0))


def attention(projected, seq_len, factor):
    images, rows, wide = projected.shape
    return pl.pallas_call(
        functools.partial(attend, seq_len, factor),
        grid=(images,),
        in_specs=[whole((rows, wide))],
        out_specs=whole((rows, wide // 3)),
        out_shape=jax.ShapeDtypeStruct((images, rows, wide // 3), jnp.bfloat16),
        compiler_params=pltpu.CompilerParams(vmem_limit_bytes=40 << 20),
    )(projected)


def attention_back(projected, back_head, seq_len, factor):
    images, rows, wide = projected.shape
    return pl.pallas_call(
        functools.partial(attend_back, seq_len, factor),
        grid=(images,),
        in_specs=[whole((rows, wide)), whole((rows, wide // 3))],
        out_specs=whole((rows, wide)),
        out_shape=jax.ShapeDtypeStruct((images, rows, wide), jnp.bfloat16),
        compiler_params=pltpu.CompilerParams(vmem_limit_bytes=40 << 20),
    )(projected, back_head)


TERMS = (0.254829592, -0.284496736, 1.421413741, -1.453152027, 1.061405429)


def gelu_and_slope(hidden):
    size = jnp.abs(hidden) * math.sqrt(0.5)
    t = 1.0 / (1.0 + 0.3275911 * size)
    bell = jnp.exp(-size * size)
    series = TERMS[4] * t + TERMS[3]
    for term in TERMS[2::-1]:
        series = series * t + term
    tail = 0.5 * series * t * bell
    below = jnp.where(hidden < 0, tail, 1.0 - tail)
    return hidden * below, below + hidden * bell * (1.0 / math.sqrt(2.0 * math.pi))


def expand(step, rows_ref, weight_ref, shift_ref, active_ref, slope_ref):
    for start in range(0, rows_ref.shape[0], step):
        at = pl.ds(start, step)
        hidden = dot(rows_ref[at, :], weight_ref[...]) + shift_ref[...]
        active, slope = gelu_and_slope(hidden)
        active_ref[at, :] = active.astype(LOW)
        slope_ref[at, :] = slope.astype(LOW)


def expanded(rows, weight, shift, step, width=512):
    count, depth = rows.shape
    full = weight.shape[1]
    out = jax.ShapeDtypeStruct((count, full), LOW)
    spec = pl.BlockSpec((count, width), lambda j: (0, j))
    return pl.pallas_call(
        functools.partial(expand, step),
        grid=(full // width,),
        in_specs=[
            pl.BlockSpec((count, depth), lambda j: (0, 0)),
            pl.BlockSpec((depth, width), lambda j: (0, j)),
            pl.BlockSpec((1, width), lambda j: (0, j)),
        ],
        out_specs=[spec, spec],
        out_shape=[out, out],
        compiler_params=pltpu.CompilerParams(vmem_limit_bytes=40 << 20),
        cost_estimate=pl.CostEstimate(
            flops=2 * count * depth * full, bytes_accessed=6 * count * full, transcendentals=2 * count * full
        ),
    )(rows, weight, shift)


def centred(values):
    center = values - jnp.mean(values, axis=-1, keepdims=True)
    rate = lax.rsqrt(jnp.mean(center * center, axis=-1, keepdims=True) + EPSILON)
    return center * rate, rate


def norm_back(values, scale, grad):
    unit, rate = centred(values)
    scaled = grad * scale
    inner = jnp.mean(scaled * unit, axis=-1, keepdims=True)
    back = rate * (scaled - jnp.mean(scaled, axis=-1, keepdims=True) - unit * inner)
    return back, jnp.sum(grad * unit, axis=0), jnp.sum(grad, axis=0)


def column_total(values):
    return jnp.sum(values.astype(WIDE), axis=0)


def per_device(
    devices,
    tokens,
    w_qkv,
    w_out,
    w_up,
    w_down,
    norm1_scale,
    norm1_offset,
    qv_bias,
    out_bias,
    norm2_scale,
    norm2_offset,
    up_bias,
    down_bias,
    cotangent,
    counts,
):
    images, seq_len, width = tokens.shape
    share = width // devices
    rows = -(-seq_len // 16) * 16
    row_count = images * rows
    factor = (width // HEADS) ** -0.5
    small = (norm1_scale, norm1_offset, qv_bias, out_bias, norm2_scale, norm2_offset, up_bias, down_bias)
    small_sizes = [v.shape[0] for v in small]

    def columns(matrix):
        return [matrix[:, at : at + width] for at in range(0, matrix.shape[1], width)]

    def small_rows(parts):
        flat = jnp.concatenate(parts, axis=-1)
        return jnp.pad(flat, [(0, 0)] * (flat.ndim - 1) + [(0, 16 * width - flat.shape[-1])]).reshape(
            flat.shape[:-1] + (16, width)
        )

    def small_split(block):
        flat, at, parts = block.reshape(block.shape[0], -1), 0, []
        for size in small_sizes:
            parts.append(flat[:, at : at + size])
            at += size
        return parts

    pack = jnp.concatenate([*columns(w_qkv), w_out, *columns(w_up), w_down, small_rows(small)], axis=0)
    whole = lax.all_gather(pack, AXES, axis=0, tiled=False)
    at = 0

    def take(count, size=share):
        nonlocal at
        parts = []
        for _ in range(count):
            parts.append(whole[:, at : at + size].reshape(devices * size, width))
            at += size
        return parts[0] if count == 1 else jnp.concatenate(parts, axis=1)

    full_qkv = take(w_qkv.shape[1] // width)
    full_out = take(1)
    full_up = take(w_up.shape[1] // width)
    full_down = take(1, w_down.shape[0])
    vectors = [v.reshape(-1).astype(WIDE) for v in small_split(whole[:, at:])]
    scale_one, offset_one, qv_full, out_shift, scale_two, offset_two, up_shift, down_shift = vectors

    def padded(array):
        return jnp.pad(array, ((0, 0), (0, rows - seq_len), (0, 0))).reshape(row_count, width)

    live = (jnp.arange(images) < counts[0])[:, None, None]
    inputs = padded(tokens).astype(WIDE)
    seed_low = padded(jnp.where(live, cotangent, jnp.zeros((), LOW)))

    normed = (centred(inputs)[0] * scale_one + offset_one).astype(LOW)
    bias_full = jnp.concatenate([qv_full[:width], jnp.zeros((width,), WIDE), qv_full[width:]])
    projected = (dot(normed, full_qkv) + bias_full).astype(LOW).reshape(images, rows, 3 * width)
    head_out = attention(projected, seq_len, factor).reshape(row_count, width)
    middle = inputs + dot(head_out, full_out) + out_shift
    normed_two = (centred(middle)[0] * scale_two + offset_two).astype(LOW)
    active, slope = expanded(normed_two, full_up, up_shift[None], rows)
    result = (middle + dot(active, full_down) + down_shift).reshape(images, rows, width)[:, :seq_len]
    out_tokens = jnp.where(live, result, 0.0).astype(LOW)

    grad_down = dot(active, seed_low, TN).astype(LOW)
    back_hidden = (dot(seed_low, full_down, NT) * slope.astype(WIDE)).astype(LOW)
    grad_up = dot(normed_two, back_hidden, TN).astype(LOW)
    back_two = dot(back_hidden, full_up, NT)
    middle_part, grad_scale_two, grad_offset_two = norm_back(middle, scale_two, back_two)
    back_middle = seed_low.astype(WIDE) + middle_part
    back_branch = back_middle.astype(LOW)
    grad_out = dot(head_out, back_branch, TN).astype(LOW)
    blocks = lambda matrix: [m.reshape(devices, -1, width) for m in columns(matrix)]
    early = jnp.concatenate([*blocks(grad_out), *blocks(grad_up), *blocks(grad_down)], axis=1)
    early = lax.psum_scatter(early, AXES, scatter_dimension=0, tiled=True)[0]

    back_head = dot(back_branch, full_out, NT).astype(LOW).reshape(images, rows, width)
    back_projected = attention_back(projected, back_head, seq_len, factor).reshape(row_count, 3 * width)
    grad_qkv = dot(normed, back_projected, TN).astype(LOW)
    back_one = dot(back_projected, full_qkv, NT)
    input_part, grad_scale_one, grad_offset_one = norm_back(inputs, scale_one, back_one)
    grad_inputs = (back_middle + input_part).reshape(images, rows, width)[:, :seq_len]
    sums = column_total(back_projected)
    small_grads = (
        grad_scale_one,
        grad_offset_one,
        jnp.concatenate([sums[:width], sums[2 * width :]]),
        column_total(back_branch),
        grad_scale_two,
        grad_offset_two,
        column_total(back_hidden),
        column_total(seed_low),
    )
    small_block = small_rows([v.astype(LOW).reshape(devices, -1) for v in small_grads])
    late = jnp.concatenate([*blocks(grad_qkv), small_block], axis=1)
    late = lax.psum_scatter(late, AXES, scatter_dimension=0, tiled=True)[0]

    def join(block, count):
        return jnp.concatenate([block[i * share : (i + 1) * share] for i in range(count)], axis=1).astype(WIDE)

    ups = w_up.shape[1] // width
    small_out = [v[0].astype(WIDE) for v in small_split(late[None, 3 * share :])]
    return (
        out_tokens,
        grad_inputs,
        join(late, 3),
        join(early, 1),
        join(early[share:], ups),
        early[share * (1 + ups) :].astype(WIDE),
        *small_out,
    )


def solution(mesh):
    split = P(AXES)
    return jax.shard_map(
        functools.partial(per_device, mesh.shape["fsdp"] * mesh.shape["dp"]),
        mesh=mesh,
        in_specs=(split,) * 15,
        out_specs=(split,) * 14,
        check_vma=False,
    )
```

```python
import functools
import math

import jax
import jax.numpy as jnp
from jax import lax
from jax.experimental import pallas as pl
from jax.experimental.pallas import tpu as pltpu
from jax.sharding import PartitionSpec as P

HEADS = 12
EPSILON = 1e-06
AXES = ("fsdp", "dp")
LOW = jnp.bfloat16
WIDE = jnp.float32
NN = (((1,), (0,)), ((), ()))
NT = (((1,), (1,)), ((), ()))
TN = (((0,), (0,)), ((), ()))


def dot(a, b, dims=NN):
    return lax.dot_general(a, b, dims, preferred_element_type=WIDE)


def attend(seq_len, factor, proj_ref, out_ref):
    rows, model_width = out_ref.shape[1:]
    lane = lax.broadcasted_iota(jnp.int32, (1, 128), 1)
    key_at = lax.broadcasted_iota(jnp.int32, (1, rows), 1)
    ones = jnp.ones((rows, 128), jnp.bfloat16)
    zero = jnp.zeros((), jnp.bfloat16)
    for pair in range(model_width // 128):
        at = pair * 128
        queries = proj_ref[0, :, at : at + 128]
        keys = proj_ref[0, :, model_width + at : model_width + at + 128]
        values = proj_ref[0, :, 2 * model_width + at : 2 * model_width + at + 128]
        wide = jnp.concatenate([values, ones], axis=1)
        halves = []
        for half in range(2):
            mine = (lane < 64) if half == 0 else (lane >= 64)
            scores = dot(jnp.where(mine, queries, zero), keys, NT)
            scores = jnp.where(key_at < seq_len, scores, -jnp.inf)
            top = jnp.max(scores, axis=1, keepdims=True)
            expo = jnp.exp((scores - top) * factor).astype(jnp.bfloat16)
            both = dot(expo, wide, NN)
            halves.append(both[:, :128] / both[:, 128:])
        out_ref[0, :, at : at + 128] = jnp.where(lane < 64, halves[0], halves[1]).astype(jnp.bfloat16)


def attend_back(seq_len, factor, proj_ref, back_ref, out_ref):
    rows, model_width = back_ref.shape[1:]
    lane = lax.broadcasted_iota(jnp.int32, (1, 128), 1)
    key_at = lax.broadcasted_iota(jnp.int32, (rows, 1), 0)
    zero = jnp.zeros((), jnp.bfloat16)
    for pair in range(model_width // 128):
        at = pair * 128
        queries = proj_ref[0, :, at : at + 128]
        keys = proj_ref[0, :, model_width + at : model_width + at + 128]
        values = proj_ref[0, :, 2 * model_width + at : 2 * model_width + at + 128]
        back = back_ref[0, :, at : at + 128]
        parts = []
        for half in range(2):
            mine = (lane < 64) if half == 0 else (lane >= 64)
            queries_one = jnp.where(mine, queries, zero)
            back_one = jnp.where(mine, back, zero)
            scores = dot(keys, queries_one, NT)
            scores = jnp.where(key_at < seq_len, scores, -jnp.inf)
            top = jnp.max(scores, axis=0, keepdims=True)
            expo = jnp.exp((scores - top) * factor)
            probs = expo * (1.0 / jnp.sum(expo, axis=0, keepdims=True))
            back_probs = dot(values, back_one, NT)
            weighted = probs * back_probs
            row_dot = jnp.sum(weighted, axis=0, keepdims=True)
            scaled = ((weighted - probs * row_dot) * factor).astype(jnp.bfloat16)
            parts.append(
                (
                    dot(scaled, keys, TN),
                    dot(scaled, queries_one, NN),
                    dot(probs.astype(jnp.bfloat16), back_one, NN),
                )
            )
        first, second = parts
        out_ref[0, :, at : at + 128] = jnp.where(lane < 64, first[0], second[0]).astype(jnp.bfloat16)
        out_ref[0, :, model_width + at : model_width + at + 128] = (first[1] + second[1]).astype(jnp.bfloat16)
        out_ref[0, :, 2 * model_width + at : 2 * model_width + at + 128] = (first[2] + second[2]).astype(jnp.bfloat16)


def whole(shape):
    return pl.BlockSpec((1,) + shape, lambda i: (i, 0, 0))


def attention(projected, seq_len, factor):
    images, rows, wide = projected.shape
    return pl.pallas_call(
        functools.partial(attend, seq_len, factor),
        grid=(images,),
        in_specs=[whole((rows, wide))],
        out_specs=whole((rows, wide // 3)),
        out_shape=jax.ShapeDtypeStruct((images, rows, wide // 3), jnp.bfloat16),
        compiler_params=pltpu.CompilerParams(vmem_limit_bytes=40 << 20),
    )(projected)


def attention_back(projected, back_head, seq_len, factor):
    images, rows, wide = projected.shape
    return pl.pallas_call(
        functools.partial(attend_back, seq_len, factor),
        grid=(images,),
        in_specs=[whole((rows, wide)), whole((rows, wide // 3))],
        out_specs=whole((rows, wide)),
        out_shape=jax.ShapeDtypeStruct((images, rows, wide), jnp.bfloat16),
        compiler_params=pltpu.CompilerParams(vmem_limit_bytes=40 << 20),
    )(projected, back_head)


TERMS = (0.254829592, -0.284496736, 1.421413741, -1.453152027, 1.061405429)


def gelu_and_slope(hidden):
    size = jnp.abs(hidden) * math.sqrt(0.5)
    t = 1.0 / (1.0 + 0.3275911 * size)
    bell = jnp.exp(-size * size)
    series = TERMS[4] * t + TERMS[3]
    for term in TERMS[2::-1]:
        series = series * t + term
    tail = 0.5 * series * t * bell
    below = jnp.where(hidden < 0, tail, 1.0 - tail)
    return hidden * below, below + hidden * bell * (1.0 / math.sqrt(2.0 * math.pi))


def expand(step, rows_ref, weight_ref, shift_ref, active_ref, slope_ref):
    for start in range(0, rows_ref.shape[0], step):
        at = pl.ds(start, step)
        hidden = dot(rows_ref[at, :], weight_ref[...]) + shift_ref[...]
        active, slope = gelu_and_slope(hidden)
        active_ref[at, :] = active.astype(LOW)
        slope_ref[at, :] = slope.astype(LOW)


def expanded(rows, weight, shift, step, width=512):
    count, depth = rows.shape
    full = weight.shape[1]
    out = jax.ShapeDtypeStruct((count, full), LOW)
    spec = pl.BlockSpec((count, width), lambda j: (0, j))
    return pl.pallas_call(
        functools.partial(expand, step),
        grid=(full // width,),
        in_specs=[
            pl.BlockSpec((count, depth), lambda j: (0, 0)),
            pl.BlockSpec((depth, width), lambda j: (0, j)),
            pl.BlockSpec((1, width), lambda j: (0, j)),
        ],
        out_specs=[spec, spec],
        out_shape=[out, out],
        compiler_params=pltpu.CompilerParams(vmem_limit_bytes=40 << 20),
        cost_estimate=pl.CostEstimate(
            flops=2 * count * depth * full, bytes_accessed=6 * count * full, transcendentals=2 * count * full
        ),
    )(rows, weight, shift)


def centred(values):
    center = values - jnp.mean(values, axis=-1, keepdims=True)
    rate = lax.rsqrt(jnp.mean(center * center, axis=-1, keepdims=True) + EPSILON)
    return center * rate, rate


def norm_back(values, scale, grad):
    unit, rate = centred(values)
    scaled = grad * scale
    inner = jnp.mean(scaled * unit, axis=-1, keepdims=True)
    back = rate * (scaled - jnp.mean(scaled, axis=-1, keepdims=True) - unit * inner)
    return back, jnp.sum(grad * unit, axis=0), jnp.sum(grad, axis=0)


def column_total(values):
    return jnp.sum(values.astype(WIDE), axis=0)


def places(sizes):
    return [(name, 1 << k) for name in AXES for k in reversed(range(sizes[name].bit_length() - 1))]


def flipped(block, name, bit, sizes):
    return lax.ppermute(block, name, [(i, i ^ bit) for i in range(sizes[name])])


def is_set(name, bit):
    return (lax.axis_index(name) & bit) != 0


def routes(sizes):
    order = places(sizes)
    far = [p for p in order if p[0] == "fsdp" and p[1] > 1]
    near = [p for p in order if p[0] == "fsdp" and p[1] == 1]
    other = [p for p in order if p[0] == "dp" and p[1] > 1]
    core = [p for p in order if p[0] == "dp" and p[1] == 1]
    return far, near + other, other + near, core


def gather_by(block, steps, done, order, sizes):
    for place in steps:
        got = flipped(block, *place, sizes)
        high = is_set(*place)
        at = sum(order.index(p) < order.index(place) for p in done)
        block = jnp.stack([jnp.where(high, got, block), jnp.where(high, block, got)], axis=at)
        done = done + [place]
    return block, done


def scatter_by(block, steps, left, sizes, kind=LOW):
    for place in steps:
        at = left.index(place)
        bit = is_set(*place).astype(jnp.int32)
        got = flipped(lax.dynamic_index_in_dim(block, 1 - bit, at, keepdims=False), *place, sizes)
        mine = lax.dynamic_index_in_dim(block, bit, at, keepdims=False)
        block = (mine.astype(WIDE) + got.astype(WIDE)).astype(kind)
        left = [p for p in left if p != place]
    return block, left


def gathered(block, sizes):
    order = places(sizes)
    far, one_way, other_way, core = routes(sizes)
    block, done = gather_by(block, far, [], order, sizes)
    half = block.shape[-1] // 2
    parts = []
    for part, way in ((block[..., :half], one_way), (block[..., half:], other_way)):
        part, _ = gather_by(part, way + core, done, order, sizes)
        parts.append(part.reshape((-1,) + part.shape[-2:]))
    return parts


def scattered(blocks, sizes):
    order = places(sizes)
    far, one_way, other_way, core = routes(sizes)
    blocks = blocks.reshape((2,) * len(order) + blocks.shape[1:])
    blocks, left = scatter_by(blocks, core, order, sizes)
    half = blocks.shape[-1] // 2
    one, rest = scatter_by(blocks[..., :half], one_way[::-1], left, sizes)
    two, rest = scatter_by(blocks[..., half:], other_way[::-1], left, sizes)
    blocks, rest = scatter_by(jnp.concatenate([one, two], axis=-1), far[:0:-1], rest, sizes)
    return scatter_by(blocks, far[:1], rest, sizes, WIDE)[0]


def scattered_small(blocks, sizes):
    order = places(sizes)
    blocks = blocks.reshape((2,) * len(order) + blocks.shape[1:])
    return scatter_by(blocks, order[::-1], order, sizes, WIDE)[0]


def per_device(
    sizes,
    tokens,
    w_qkv,
    w_out,
    w_up,
    w_down,
    norm1_scale,
    norm1_offset,
    qv_bias,
    out_bias,
    norm2_scale,
    norm2_offset,
    up_bias,
    down_bias,
    cotangent,
    counts,
):
    devices = sizes["fsdp"] * sizes["dp"]
    images, seq_len, width = tokens.shape
    share = width // devices
    rows = -(-seq_len // 16) * 16
    row_count = images * rows
    factor = (width // HEADS) ** -0.5
    small = (norm1_scale, norm1_offset, qv_bias, out_bias, norm2_scale, norm2_offset, up_bias, down_bias)
    small_sizes = [v.shape[0] for v in small]

    def columns(matrix):
        return [matrix[:, at : at + width] for at in range(0, matrix.shape[1], width)]

    def small_rows(parts):
        flat = jnp.concatenate(parts, axis=-1)
        return jnp.pad(flat, [(0, 0)] * (flat.ndim - 1) + [(0, 8 * width - flat.shape[-1])]).reshape(
            flat.shape[:-1] + (8, width)
        )

    def small_split(block):
        flat, at, parts = block.reshape(block.shape[0], -1), 0, []
        for size in small_sizes:
            parts.append(flat[:, at : at + size])
            at += size
        return parts

    first = jnp.concatenate([*columns(w_qkv), small_rows(small)], axis=0)
    first_left, first_right = gathered(first, sizes)
    qkv_parts = []
    for i in range(3):
        for part in (first_left, first_right):
            qkv_parts.append(part[:, i * share : (i + 1) * share].reshape(width, width // 2))
    full_qkv = jnp.concatenate(qkv_parts, axis=1)
    rest = jnp.concatenate([w_out, *columns(w_up), w_down], axis=0)
    whole = lax.all_gather(rest, AXES, axis=0, tiled=False)
    at = 0

    def take(count, size=share):
        nonlocal at
        parts = []
        for _ in range(count):
            parts.append(whole[:, at : at + size].reshape(devices * size, width))
            at += size
        return parts[0] if count == 1 else jnp.concatenate(parts, axis=1)

    full_out = take(1)
    full_up = take(w_up.shape[1] // width)
    full_down = take(1, w_down.shape[0])
    vectors = [v.reshape(-1).astype(WIDE) for v in small_split(first_left[:, 3 * share :])]
    scale_one, offset_one, qv_full, out_shift, scale_two, offset_two, up_shift, down_shift = vectors

    def padded(array):
        return jnp.pad(array, ((0, 0), (0, rows - seq_len), (0, 0))).reshape(row_count, width)

    live = (jnp.arange(images) < counts[0])[:, None, None]
    inputs = padded(tokens).astype(WIDE)
    seed_low = padded(jnp.where(live, cotangent, jnp.zeros((), LOW)))

    normed = (centred(inputs)[0] * scale_one + offset_one).astype(LOW)
    bias_full = jnp.concatenate([qv_full[:width], jnp.zeros((width,), WIDE), qv_full[width:]])
    projected = (dot(normed, full_qkv) + bias_full).astype(LOW).reshape(images, rows, 3 * width)
    head_out = attention(projected, seq_len, factor).reshape(row_count, width)
    middle = inputs + dot(head_out, full_out) + out_shift
    normed_two = (centred(middle)[0] * scale_two + offset_two).astype(LOW)
    active, slope = expanded(normed_two, full_up, up_shift[None], rows)
    result = (middle + dot(active, full_down) + down_shift).reshape(images, rows, width)[:, :seq_len]
    out_tokens = jnp.where(live, result, 0.0).astype(LOW)

    grad_down = dot(active, seed_low, TN).astype(LOW)
    back_hidden = (dot(seed_low, full_down, NT) * slope.astype(WIDE)).astype(LOW)
    grad_up = dot(normed_two, back_hidden, TN).astype(LOW)
    back_two = dot(back_hidden, full_up, NT)
    middle_part, grad_scale_two, grad_offset_two = norm_back(middle, scale_two, back_two)
    back_middle = seed_low.astype(WIDE) + middle_part
    back_branch = back_middle.astype(LOW)
    grad_out = dot(head_out, back_branch, TN).astype(LOW)
    blocks = lambda matrix: [m.reshape(devices, -1, width) for m in columns(matrix)]
    early = jnp.concatenate([*blocks(grad_out), *blocks(grad_up), *blocks(grad_down)], axis=1)
    early = lax.psum_scatter(early, AXES, scatter_dimension=0, tiled=True)[0]

    back_head = dot(back_branch, full_out, NT).astype(LOW).reshape(images, rows, width)
    back_projected = attention_back(projected, back_head, seq_len, factor).reshape(row_count, 3 * width)
    grad_qkv = dot(normed, back_projected, TN).astype(LOW)
    back_one = dot(back_projected, full_qkv, NT)
    input_part, grad_scale_one, grad_offset_one = norm_back(inputs, scale_one, back_one)
    grad_inputs = (back_middle + input_part).reshape(images, rows, width)[:, :seq_len]
    sums = column_total(back_projected)
    small_grads = (
        grad_scale_one,
        grad_offset_one,
        jnp.concatenate([sums[:width], sums[2 * width :]]),
        column_total(back_branch),
        grad_scale_two,
        grad_offset_two,
        column_total(back_hidden),
        column_total(seed_low),
    )
    small_block = small_rows([v.reshape(devices, -1) for v in small_grads])[:, :1]
    small_sum = scattered_small(small_block, sizes)
    late = scattered(jnp.concatenate(blocks(grad_qkv), axis=1), sizes)

    def join(block, count):
        return jnp.concatenate([block[i * share : (i + 1) * share] for i in range(count)], axis=1).astype(WIDE)

    ups = w_up.shape[1] // width
    small_out = [v[0] for v in small_split(small_sum[None])]
    return (
        out_tokens,
        grad_inputs,
        join(late, 3),
        join(early, 1),
        join(early[share:], ups),
        early[share * (1 + ups) :].astype(WIDE),
        *small_out,
    )


def solution(mesh):
    split = P(AXES)
    return jax.shard_map(
        functools.partial(per_device, dict(mesh.shape)),
        mesh=mesh,
        in_specs=(split,) * 15,
        out_specs=(split,) * 14,
        check_vma=False,
    )
```

```python
import functools
import math

import jax
import jax.numpy as jnp
from jax import lax
from jax.experimental import pallas as pl
from jax.experimental.pallas import tpu as pltpu
from jax.sharding import PartitionSpec as P

HEADS = 12
EPSILON = 1e-06
AXES = ("fsdp", "dp")
LOW = jnp.bfloat16
WIDE = jnp.float32
NN = (((1,), (0,)), ((), ()))
NT = (((1,), (1,)), ((), ()))
TN = (((0,), (0,)), ((), ()))


def dot(a, b, dims=NN):
    return lax.dot_general(a, b, dims, preferred_element_type=WIDE)


def attend(seq_len, factor, proj_ref, out_ref):
    rows, model_width = out_ref.shape[1:]
    lane = lax.broadcasted_iota(jnp.int32, (1, 128), 1)
    key_at = lax.broadcasted_iota(jnp.int32, (1, rows), 1)
    ones = jnp.ones((rows, 128), jnp.bfloat16)
    zero = jnp.zeros((), jnp.bfloat16)
    for pair in range(model_width // 128):
        at = pair * 128
        queries = proj_ref[0, :, at : at + 128]
        keys = proj_ref[0, :, model_width + at : model_width + at + 128]
        values = proj_ref[0, :, 2 * model_width + at : 2 * model_width + at + 128]
        wide = jnp.concatenate([values, ones], axis=1)
        halves = []
        for half in range(2):
            mine = (lane < 64) if half == 0 else (lane >= 64)
            scores = dot(jnp.where(mine, queries, zero), keys, NT)
            scores = jnp.where(key_at < seq_len, scores, -jnp.inf)
            top = jnp.max(scores, axis=1, keepdims=True)
            expo = jnp.exp((scores - top) * factor).astype(jnp.bfloat16)
            both = dot(expo, wide, NN)
            halves.append(both[:, :128] / both[:, 128:])
        out_ref[0, :, at : at + 128] = jnp.where(lane < 64, halves[0], halves[1]).astype(jnp.bfloat16)


def attend_back(seq_len, factor, proj_ref, back_ref, *refs):
    out_ref = refs[-1]
    rows, model_width = back_ref.shape[1:]
    lane = lax.broadcasted_iota(jnp.int32, (1, 128), 1)
    key_at = lax.broadcasted_iota(jnp.int32, (rows, 1), 0)
    zero = jnp.zeros((), jnp.bfloat16)
    for pair in range(model_width // 128):
        at = pair * 128
        queries = proj_ref[0, :, at : at + 128]
        keys = proj_ref[0, :, model_width + at : model_width + at + 128]
        values = proj_ref[0, :, 2 * model_width + at : 2 * model_width + at + 128]
        back = back_ref[0, :, at : at + 128]
        parts = []
        for half in range(2):
            mine = (lane < 64) if half == 0 else (lane >= 64)
            queries_one = jnp.where(mine, queries, zero)
            back_one = jnp.where(mine, back, zero)
            scores = dot(keys, queries_one, NT)
            scores = jnp.where(key_at < seq_len, scores, -jnp.inf)
            top = jnp.max(scores, axis=0, keepdims=True)
            expo = jnp.exp((scores - top) * factor)
            probs = expo * (1.0 / jnp.sum(expo, axis=0, keepdims=True))
            back_probs = dot(values, back_one, NT)
            weighted = probs * back_probs
            row_dot = jnp.sum(weighted, axis=0, keepdims=True)
            scaled = ((weighted - probs * row_dot) * factor).astype(jnp.bfloat16)
            parts.append(
                (
                    dot(scaled, keys, TN),
                    dot(scaled, queries_one, NN),
                    dot(probs.astype(jnp.bfloat16), back_one, NN),
                )
            )
        first, second = parts
        out_ref[0, :, at : at + 128] = jnp.where(lane < 64, first[0], second[0]).astype(jnp.bfloat16)
        out_ref[0, :, model_width + at : model_width + at + 128] = (first[1] + second[1]).astype(jnp.bfloat16)
        out_ref[0, :, 2 * model_width + at : 2 * model_width + at + 128] = (first[2] + second[2]).astype(jnp.bfloat16)


def whole(shape):
    return pl.BlockSpec((1,) + shape, lambda i: (i, 0, 0))


def attention(projected, seq_len, factor):
    images, rows, wide = projected.shape
    return pl.pallas_call(
        functools.partial(attend, seq_len, factor),
        grid=(images,),
        in_specs=[whole((rows, wide))],
        out_specs=whole((rows, wide // 3)),
        out_shape=jax.ShapeDtypeStruct((images, rows, wide // 3), jnp.bfloat16),
        compiler_params=pltpu.CompilerParams(vmem_limit_bytes=40 << 20),
    )(projected)


def attention_back(projected, back_head, seq_len, factor, group):
    images, rows, wide = projected.shape
    done = None
    for start in range(0, images, group):
        def block(shape, start=start):
            return pl.BlockSpec((1,) + shape, lambda i: (i + start, 0, 0))

        kept = () if done is None else (done,)
        done = pl.pallas_call(
            functools.partial(attend_back, seq_len, factor),
            grid=(min(group, images - start),),
            in_specs=[block((rows, wide)), block((rows, wide // 3))] + [pl.BlockSpec(memory_space=pl.ANY)] * len(kept),
            out_specs=block((rows, wide)),
            out_shape=jax.ShapeDtypeStruct((images, rows, wide), jnp.bfloat16),
            input_output_aliases={2: 0} if kept else {},
            compiler_params=pltpu.CompilerParams(vmem_limit_bytes=40 << 20),
            cost_estimate=pl.CostEstimate(
                flops=group * HEADS * 10 * rows * rows * 256, bytes_accessed=14 * group * rows * wide, transcendentals=0
            ),
        )(projected, back_head, *kept)
    return done


TERMS = (0.254829592, -0.284496736, 1.421413741, -1.453152027, 1.061405429)


def gelu_and_slope(hidden):
    size = jnp.abs(hidden) * math.sqrt(0.5)
    t = 1.0 / (1.0 + 0.3275911 * size)
    bell = jnp.exp(-size * size)
    series = TERMS[4] * t + TERMS[3]
    for term in TERMS[2::-1]:
        series = series * t + term
    tail = 0.5 * series * t * bell
    below = jnp.where(hidden < 0, tail, 1.0 - tail)
    return hidden * below, below + hidden * bell * (1.0 / math.sqrt(2.0 * math.pi))


def expand(step, rows_ref, weight_ref, shift_ref, active_ref, slope_ref):
    for start in range(0, rows_ref.shape[0], step):
        at = pl.ds(start, step)
        hidden = dot(rows_ref[at, :], weight_ref[...]) + shift_ref[...]
        active, slope = gelu_and_slope(hidden)
        active_ref[at, :] = active.astype(LOW)
        slope_ref[at, :] = slope.astype(LOW)


def expanded(rows, weight, shift, step, width=512):
    count, depth = rows.shape
    full = shift.shape[1]
    out = jax.ShapeDtypeStruct((count, full), LOW)
    spec = pl.BlockSpec((count, width), lambda j: (0, j))
    return pl.pallas_call(
        functools.partial(expand, step),
        grid=(full // width,),
        in_specs=[
            pl.BlockSpec((count, depth), lambda j: (0, 0)),
            pl.BlockSpec((depth, width), lambda j: (0, j)),
            pl.BlockSpec((1, width), lambda j: (0, j)),
        ],
        out_specs=[spec, spec],
        out_shape=[out, out],
        compiler_params=pltpu.CompilerParams(vmem_limit_bytes=40 << 20),
        cost_estimate=pl.CostEstimate(
            flops=2 * count * depth * full, bytes_accessed=6 * count * full, transcendentals=2 * count * full
        ),
    )(rows, weight, shift)


def centred(values):
    center = values - jnp.mean(values, axis=-1, keepdims=True)
    rate = lax.rsqrt(jnp.mean(center * center, axis=-1, keepdims=True) + EPSILON)
    return center * rate, rate


def norm_back(values, scale, grad):
    unit, rate = centred(values)
    scaled = grad * scale
    inner = jnp.mean(scaled * unit, axis=-1, keepdims=True)
    back = rate * (scaled - jnp.mean(scaled, axis=-1, keepdims=True) - unit * inner)
    return back, jnp.sum(grad * unit, axis=0), jnp.sum(grad, axis=0)


def column_total(values):
    return jnp.sum(values.astype(WIDE), axis=0)


def places(sizes):
    return [(name, 1 << k) for name in AXES for k in reversed(range(sizes[name].bit_length() - 1))]


def flipped(block, name, bit, sizes):
    return lax.ppermute(block, name, [(i, i ^ bit) for i in range(sizes[name])])


def is_set(name, bit):
    return (lax.axis_index(name) & bit) != 0


def routes(sizes):
    order = places(sizes)
    far = [p for p in order if p[0] == "fsdp" and p[1] > 1]
    near = [p for p in order if p[0] == "fsdp" and p[1] == 1]
    other = [p for p in order if p[0] == "dp" and p[1] > 1]
    core = [p for p in order if p[0] == "dp" and p[1] == 1]
    return far, near + other, other + near, core


def gather_by(block, steps, done, order, sizes):
    for place in steps:
        got = flipped(block, *place, sizes)
        high = is_set(*place)
        at = sum(order.index(p) < order.index(place) for p in done)
        block = jnp.stack([jnp.where(high, got, block), jnp.where(high, block, got)], axis=at)
        done = done + [place]
    return block, done


def scatter_by(block, steps, left, sizes, kind=LOW):
    for place in steps:
        at = left.index(place)
        bit = is_set(*place).astype(jnp.int32)
        got = flipped(lax.dynamic_index_in_dim(block, 1 - bit, at, keepdims=False), *place, sizes)
        mine = lax.dynamic_index_in_dim(block, bit, at, keepdims=False)
        block = (mine.astype(WIDE) + got.astype(WIDE)).astype(kind)
        left = [p for p in left if p != place]
    return block, left


def gathered(block, half, sizes):
    order = places(sizes)
    far, one_way, other_way, core = routes(sizes)
    block, done = gather_by(block, far, [], order, sizes)
    parts = []
    for part, way in ((block[..., :half], one_way), (block[..., half:], other_way)):
        part, _ = gather_by(part, way + core, done, order, sizes)
        parts.append(part.reshape(-1, part.shape[-1]))
    return parts


def scattered(arrays, sizes):
    order = places(sizes)
    far, one_way, other_way, core = routes(sizes)
    bit = is_set(*core[0]).astype(jnp.int32)

    def half_of(at):
        cut = [a.reshape((-1, 2, a.shape[0] // (1 << len(order)), a.shape[1])) for a in arrays]
        cut = [lax.dynamic_index_in_dim(a, at, 1, keepdims=False) for a in cut]
        return jnp.concatenate(cut, axis=-1)

    got = flipped(half_of(1 - bit), *core[0], sizes)
    blocks = (half_of(bit).astype(WIDE) + got.astype(WIDE)).astype(LOW)
    left = order[:-1]
    blocks = blocks.reshape((2,) * len(left) + blocks.shape[1:])
    half = blocks.shape[-1] // 2
    one, rest = scatter_by(blocks[..., :half], one_way[::-1], left, sizes)
    two, rest = scatter_by(blocks[..., half:], other_way[::-1], left, sizes)
    blocks, rest = scatter_by(jnp.concatenate([one, two], axis=-1), far[:0:-1], rest, sizes)
    return scatter_by(blocks, far[:1], rest, sizes, WIDE)[0]


def scattered_small(blocks, sizes):
    order = places(sizes)
    blocks = blocks.reshape((2,) * len(order) + blocks.shape[1:])
    return scatter_by(blocks, order[::-1], order, sizes, WIDE)[0]


def per_device(
    sizes,
    tokens,
    w_qkv,
    w_out,
    w_up,
    w_down,
    norm1_scale,
    norm1_offset,
    qv_bias,
    out_bias,
    norm2_scale,
    norm2_offset,
    up_bias,
    down_bias,
    cotangent,
    counts,
):
    devices = sizes["fsdp"] * sizes["dp"]
    images, seq_len, width = tokens.shape
    share = width // devices
    rows = -(-seq_len // 16) * 16
    row_count = images * rows
    factor = (width // HEADS) ** -0.5
    small = (norm1_scale, norm1_offset, qv_bias, out_bias, norm2_scale, norm2_offset, up_bias, down_bias)
    small_sizes = [v.shape[0] for v in small]

    side = -(-sum(small_sizes) // 128)

    def small_split(flat):
        at, parts = 0, []
        for size in small_sizes:
            parts.append(flat[:, at : at + size])
            at += size
        return parts

    def small_join(parts):
        total, at = 0, 0
        for part in parts:
            size = part.shape[-1]
            ends = [(0, 0)] * (part.ndim - 1) + [(at, side * 128 - at - size)]
            total = total + jnp.pad(part, ends)
            at += size
        return total

    first = [w_qkv, jnp.pad(small_join(small).reshape(side, 128), ((0, share - side), (0, 0)))]
    left, right = gathered(jnp.concatenate(first, axis=1), 3 * width // 2, sizes)
    full_qkv = jnp.concatenate([left, right[:, : 3 * width // 2]], axis=1)
    small_whole = right[:, 3 * width // 2 :].reshape(devices, share, 128)[:, :side].reshape(devices, -1)
    vectors = [v.reshape(-1).astype(WIDE) for v in small_split(small_whole)]
    scale_one, offset_one, qv_full, out_shift, scale_two, offset_two, up_shift, down_shift = vectors
    hidden_width = w_up.shape[1]
    ratio = hidden_width // width
    rest = [w_up, w_out, *[w_down[i * share : (i + 1) * share] for i in range(ratio)]]
    whole = lax.all_gather(jnp.concatenate(rest, axis=1), AXES, axis=0, tiled=True)
    full_up = whole[:, :hidden_width]
    full_out = whole[:, hidden_width : hidden_width + width]
    full_down = whole[:, hidden_width + width :].reshape(devices, share, ratio, width)
    full_down = full_down.swapaxes(1, 2).reshape(hidden_width, width)

    def padded(array):
        return jnp.pad(array, ((0, 0), (0, rows - seq_len), (0, 0))).reshape(row_count, width)

    live = (jnp.arange(images) < counts[0])[:, None, None]
    inputs = padded(tokens).astype(WIDE)
    seed_low = padded(jnp.where(live, cotangent, jnp.zeros((), LOW)))

    normed = (centred(inputs)[0] * scale_one + offset_one).astype(LOW)
    bias_full = jnp.concatenate([qv_full[:width], jnp.zeros((width,), WIDE), qv_full[width:]])
    projected = (dot(normed, full_qkv) + bias_full).astype(LOW).reshape(images, rows, 3 * width)
    head_out = attention(projected, seq_len, factor).reshape(row_count, width)
    middle = inputs + dot(head_out, full_out) + out_shift
    normed_two = (centred(middle)[0] * scale_two + offset_two).astype(LOW)
    active, slope = expanded(normed_two, whole, up_shift[None], rows)
    result = (middle + dot(active, full_down) + down_shift).reshape(images, rows, width)[:, :seq_len]
    out_tokens = jnp.where(live, result, 0.0).astype(LOW)

    grad_down = dot(active, seed_low, TN).astype(LOW)
    seed_again, grad_down = lax.optimization_barrier((seed_low, grad_down))
    down_sum = lax.psum_scatter(grad_down, AXES, scatter_dimension=0, tiled=True)
    back_hidden = (dot(seed_again, full_down, NT) * slope.astype(WIDE)).astype(LOW)
    grad_up = dot(normed_two, back_hidden, TN).astype(LOW)
    back_hidden, grad_up = lax.optimization_barrier((back_hidden, grad_up))
    up_sum = scattered([grad_up], sizes)
    back_two = dot(back_hidden, full_up, NT)
    middle_part, grad_scale_two, grad_offset_two = norm_back(middle, scale_two, back_two)
    back_middle = seed_low.astype(WIDE) + middle_part
    back_branch = back_middle.astype(LOW)
    grad_out = dot(head_out, back_branch, TN).astype(LOW)

    back_head = dot(back_branch, full_out, NT).astype(LOW).reshape(images, rows, width)
    back_projected = attention_back(projected, back_head, seq_len, factor, 2).reshape(row_count, 3 * width)
    grad_qkv = dot(normed, back_projected, TN).astype(LOW)
    back_projected, grad_qkv = lax.optimization_barrier((back_projected, grad_qkv))
    late = scattered([grad_qkv, grad_out], sizes)
    back_one = dot(back_projected, full_qkv, NT)
    input_part, grad_scale_one, grad_offset_one = norm_back(inputs, scale_one, back_one)
    grad_inputs = (back_middle + input_part).reshape(images, rows, width)[:, :seq_len]
    sums = column_total(back_projected)
    small_grads = (
        grad_scale_one,
        grad_offset_one,
        jnp.concatenate([sums[:width], sums[2 * width :]]),
        column_total(back_branch),
        grad_scale_two,
        grad_offset_two,
        column_total(back_hidden),
        column_total(seed_low),
    )
    small_sum = scattered_small(small_join([v.reshape(devices, -1) for v in small_grads]), sizes)
    small_out = [v[0] for v in small_split(small_sum[None])]
    return (
        out_tokens,
        grad_inputs,
        late[:, : 3 * width],
        late[:, 3 * width :],
        up_sum,
        down_sum.astype(WIDE),
        *small_out,
    )


def solution(mesh):
    split = P(AXES)
    return jax.shard_map(
        functools.partial(per_device, dict(mesh.shape)),
        mesh=mesh,
        in_specs=(split,) * 15,
        out_specs=(split,) * 14,
        check_vma=False,
    )
```

```python
import functools
import math

import jax
import jax.numpy as jnp
from jax import lax
from jax.experimental import pallas as pl
from jax.experimental.pallas import tpu as pltpu
from jax.sharding import PartitionSpec as P

HEADS = 12
EPSILON = 1e-06
AXES = ("fsdp", "dp")
LOW = jnp.bfloat16
WIDE = jnp.float32
NN = (((1,), (0,)), ((), ()))
NT = (((1,), (1,)), ((), ()))
TN = (((0,), (0,)), ((), ()))


def dot(a, b, dims=NN):
    return lax.dot_general(a, b, dims, preferred_element_type=WIDE)


def attend(seq_len, factor, proj_ref, out_ref):
    rows, model_width = out_ref.shape[1:]
    lane = lax.broadcasted_iota(jnp.int32, (1, 128), 1)
    key_at = lax.broadcasted_iota(jnp.int32, (1, rows), 1)
    ones = jnp.ones((rows, 128), jnp.bfloat16)
    zero = jnp.zeros((), jnp.bfloat16)
    for pair in range(model_width // 128):
        at = pair * 128
        queries = proj_ref[0, :, at : at + 128]
        keys = proj_ref[0, :, model_width + at : model_width + at + 128]
        values = proj_ref[0, :, 2 * model_width + at : 2 * model_width + at + 128]
        wide = jnp.concatenate([values, ones], axis=1)
        halves = []
        for half in range(2):
            mine = (lane < 64) if half == 0 else (lane >= 64)
            scores = dot(jnp.where(mine, queries, zero), keys, NT)
            scores = jnp.where(key_at < seq_len, scores, -jnp.inf)
            top = jnp.max(scores, axis=1, keepdims=True)
            expo = jnp.exp((scores - top) * factor).astype(jnp.bfloat16)
            both = dot(expo, wide, NN)
            halves.append(both[:, :128] / both[:, 128:])
        out_ref[0, :, at : at + 128] = jnp.where(lane < 64, halves[0], halves[1]).astype(jnp.bfloat16)


def attend_back(seq_len, factor, proj_ref, back_ref, *refs):
    out_ref = refs[-1]
    rows, model_width = back_ref.shape[1:]
    lane = lax.broadcasted_iota(jnp.int32, (1, 128), 1)
    key_at = lax.broadcasted_iota(jnp.int32, (rows, 1), 0)
    zero = jnp.zeros((), jnp.bfloat16)
    for pair in range(model_width // 128):
        at = pair * 128
        queries = proj_ref[0, :, at : at + 128]
        keys = proj_ref[0, :, model_width + at : model_width + at + 128]
        values = proj_ref[0, :, 2 * model_width + at : 2 * model_width + at + 128]
        back = back_ref[0, :, at : at + 128]
        parts = []
        for half in range(2):
            mine = (lane < 64) if half == 0 else (lane >= 64)
            queries_one = jnp.where(mine, queries, zero)
            back_one = jnp.where(mine, back, zero)
            scores = dot(keys, queries_one, NT)
            scores = jnp.where(key_at < seq_len, scores, -jnp.inf)
            top = jnp.max(scores, axis=0, keepdims=True)
            expo = jnp.exp((scores - top) * factor)
            probs = expo * (1.0 / jnp.sum(expo, axis=0, keepdims=True))
            back_probs = dot(values, back_one, NT)
            weighted = probs * back_probs
            row_dot = jnp.sum(weighted, axis=0, keepdims=True)
            scaled = ((weighted - probs * row_dot) * factor).astype(jnp.bfloat16)
            parts.append(
                (
                    dot(scaled, keys, TN),
                    dot(scaled, queries_one, NN),
                    dot(probs.astype(jnp.bfloat16), back_one, NN),
                )
            )
        first, second = parts
        out_ref[0, :, at : at + 128] = jnp.where(lane < 64, first[0], second[0]).astype(jnp.bfloat16)
        out_ref[0, :, model_width + at : model_width + at + 128] = (first[1] + second[1]).astype(jnp.bfloat16)
        out_ref[0, :, 2 * model_width + at : 2 * model_width + at + 128] = (first[2] + second[2]).astype(jnp.bfloat16)


def whole(shape):
    return pl.BlockSpec((1,) + shape, lambda i: (i, 0, 0))


def attention(projected, seq_len, factor):
    images, rows, wide = projected.shape
    return pl.pallas_call(
        functools.partial(attend, seq_len, factor),
        grid=(images,),
        in_specs=[whole((rows, wide))],
        out_specs=whole((rows, wide // 3)),
        out_shape=jax.ShapeDtypeStruct((images, rows, wide // 3), jnp.bfloat16),
        compiler_params=pltpu.CompilerParams(vmem_limit_bytes=40 << 20),
    )(projected)


def attention_back(projected, back_head, seq_len, factor, group, ties):
    images, rows, wide = projected.shape
    done = None
    for start in range(0, images, group):
        def block(shape, start=start):
            return pl.BlockSpec((1,) + shape, lambda i: (i + start, 0, 0))

        if ties.get(start):
            back_head = ties[start](back_head)
        kept = () if done is None else (done,)
        done = pl.pallas_call(
            functools.partial(attend_back, seq_len, factor),
            grid=(min(group, images - start),),
            in_specs=[block((rows, wide)), block((rows, wide // 3))] + [pl.BlockSpec(memory_space=pl.ANY)] * len(kept),
            out_specs=block((rows, wide)),
            out_shape=jax.ShapeDtypeStruct((images, rows, wide), jnp.bfloat16),
            input_output_aliases={2: 0} if kept else {},
            compiler_params=pltpu.CompilerParams(vmem_limit_bytes=40 << 20),
            cost_estimate=pl.CostEstimate(
                flops=group * HEADS * 10 * rows * rows * 256, bytes_accessed=14 * group * rows * wide, transcendentals=0
            ),
        )(projected, back_head, *kept)
    return done


TERMS = (0.254829592, -0.284496736, 1.421413741, -1.453152027, 1.061405429)


def gelu_and_slope(hidden):
    size = jnp.abs(hidden) * math.sqrt(0.5)
    t = 1.0 / (1.0 + 0.3275911 * size)
    bell = jnp.exp(-size * size)
    series = TERMS[4] * t + TERMS[3]
    for term in TERMS[2::-1]:
        series = series * t + term
    tail = 0.5 * series * t * bell
    below = jnp.where(hidden < 0, tail, 1.0 - tail)
    return hidden * below, below + hidden * bell * (1.0 / math.sqrt(2.0 * math.pi))


def expand(step, rows_ref, weight_ref, shift_ref, active_ref, slope_ref):
    for start in range(0, rows_ref.shape[0], step):
        at = pl.ds(start, step)
        hidden = dot(rows_ref[at, :], weight_ref[...]) + shift_ref[...]
        active, slope = gelu_and_slope(hidden)
        active_ref[at, :] = active.astype(LOW)
        slope_ref[at, :] = slope.astype(LOW)


def expanded(rows, weight, shift, step, width=512):
    count, depth = rows.shape
    full = shift.shape[1]
    out = jax.ShapeDtypeStruct((count, full), LOW)
    spec = pl.BlockSpec((count, width), lambda j: (0, j))
    return pl.pallas_call(
        functools.partial(expand, step),
        grid=(full // width,),
        in_specs=[
            pl.BlockSpec((count, depth), lambda j: (0, 0)),
            pl.BlockSpec((depth, width), lambda j: (0, j)),
            pl.BlockSpec((1, width), lambda j: (0, j)),
        ],
        out_specs=[spec, spec],
        out_shape=[out, out],
        compiler_params=pltpu.CompilerParams(vmem_limit_bytes=40 << 20),
        cost_estimate=pl.CostEstimate(
            flops=2 * count * depth * full, bytes_accessed=6 * count * full, transcendentals=2 * count * full
        ),
    )(rows, weight, shift)


def centred(values):
    center = values - jnp.mean(values, axis=-1, keepdims=True)
    rate = lax.rsqrt(jnp.mean(center * center, axis=-1, keepdims=True) + EPSILON)
    return center * rate, rate


def norm_back(values, scale, grad):
    unit, rate = centred(values)
    scaled = grad * scale
    inner = jnp.mean(scaled * unit, axis=-1, keepdims=True)
    back = rate * (scaled - jnp.mean(scaled, axis=-1, keepdims=True) - unit * inner)
    return back, jnp.sum(grad * unit, axis=0), jnp.sum(grad, axis=0)


def column_total(values):
    return jnp.sum(values.astype(WIDE), axis=0)


def places(sizes):
    return [(name, 1 << k) for name in AXES for k in reversed(range(sizes[name].bit_length() - 1))]


def flipped(block, name, bit, sizes):
    return lax.ppermute(block, name, [(i, i ^ bit) for i in range(sizes[name])])


def is_set(name, bit):
    return (lax.axis_index(name) & bit) != 0


def routes(sizes):
    order = places(sizes)
    far = [p for p in order if p[0] == "fsdp" and p[1] > 1]
    near = [p for p in order if p[0] == "fsdp" and p[1] == 1]
    other = [p for p in order if p[0] == "dp" and p[1] > 1]
    core = [p for p in order if p[0] == "dp" and p[1] == 1]
    return far, near + other, other + near, core


def gather_by(block, steps, done, order, sizes):
    for place in steps:
        got = flipped(block, *place, sizes)
        high = is_set(*place)
        at = sum(order.index(p) < order.index(place) for p in done)
        block = jnp.stack([jnp.where(high, got, block), jnp.where(high, block, got)], axis=at)
        done = done + [place]
    return block, done


def gathered(block, half, sizes):
    order = places(sizes)
    far, one_way, other_way, core = routes(sizes)
    block, done = gather_by(block, far, [], order, sizes)
    parts = []
    for part, way in ((block[..., :half], one_way), (block[..., half:], other_way)):
        part, _ = gather_by(part, way + core, done, order, sizes)
        parts.append(part.reshape(-1, part.shape[-1]))
    return parts


def halved(block, place, left, sizes, kind=LOW):
    at = left.index(place)
    bit = is_set(*place).astype(jnp.int32)
    got = flipped(lax.dynamic_index_in_dim(block, 1 - bit, at, keepdims=False), *place, sizes)
    mine = lax.dynamic_index_in_dim(block, bit, at, keepdims=False)
    return (mine.astype(WIDE) + got.astype(WIDE)).astype(kind)


class Scatter:
    def __init__(self, arrays, way, sizes):
        far, one_way, other_way, core = routes(sizes)
        self.sizes = sizes
        self.left = places(sizes)
        self.plan = core + (one_way, other_way)[way][::-1] + far[::-1]
        self.block = None
        place = self.plan[0]
        bit = is_set(*place).astype(jnp.int32)
        cut = [a.reshape((-1, 2, a.shape[0] >> len(self.left), a.shape[1])) for a in arrays]

        def half_of(at):
            return jnp.concatenate([lax.dynamic_index_in_dim(a, at, 1, keepdims=False) for a in cut], axis=-1)

        self.theirs = half_of(1 - bit)
        self.mine = half_of(bit)

    def step(self):
        if not self.plan:
            return
        place, self.plan = self.plan[0], self.plan[1:]
        if self.block is None:
            got = flipped(self.theirs, *place, self.sizes)
            block = (self.mine.astype(WIDE) + got.astype(WIDE)).astype(LOW)
            self.block = block.reshape((2,) * (len(self.left) - 1) + block.shape[1:])
        else:
            self.block = halved(self.block, place, self.left, self.sizes, LOW if self.plan else WIDE)
        self.left = [q for q in self.left if q != place]

    def step_and_tie(self, value):
        self.step()
        value, self.block = lax.optimization_barrier((value, self.block))
        return value

    def cut_and_tie(self, value):
        value, self.theirs = lax.optimization_barrier((value, self.theirs))
        return value

    def result(self):
        while self.plan:
            self.step()
        return self.block


def lay_out(sizes_of, block_ref, out_ref):
    devices = block_ref.shape[0]
    shares = block_ref[...].astype(WIDE)
    at, to = 0, 0
    for size in sizes_of:
        full = devices * size
        row = lax.broadcasted_iota(jnp.int32, (block_ref.shape[1], full), 0)
        column = lax.broadcasted_iota(jnp.int32, (block_ref.shape[1], full), 1)
        pick = jnp.where(row == at + lax.rem(column, size), 1.0, 0.0).astype(LOW)
        spread = dot(shares.astype(LOW), pick)
        device = lax.broadcasted_iota(jnp.int32, (devices, full), 0)
        own = lax.div(lax.broadcasted_iota(jnp.int32, (devices, full), 1), size)
        out_ref[:, to : to + full] = jnp.sum(jnp.where(device == own, spread, 0.0), axis=0, keepdims=True)
        at += size
        to += full


def laid_out(block, sizes_of):
    full = block.shape[0] * sum(sizes_of)
    flat = pl.pallas_call(
        functools.partial(lay_out, sizes_of),
        out_shape=jax.ShapeDtypeStruct((1, full), WIDE),
        compiler_params=pltpu.CompilerParams(vmem_limit_bytes=40 << 20),
    )(block)
    parts, at = [], 0
    for size in sizes_of:
        parts.append(flat[:, at : at + block.shape[0] * size])
        at += block.shape[0] * size
    return parts


def put_beside(up_ref, down_ref, out_ref):
    share, hidden_width = up_ref.shape
    width = down_ref.shape[1]
    out_ref[:, :hidden_width] = up_ref[...]
    down = down_ref[...].astype(WIDE)
    for i in range(down.shape[0] // share):
        to = hidden_width + i * width
        out_ref[:, to : to + width] = down[i * share : (i + 1) * share].astype(LOW)


def beside(up, down):
    return pl.pallas_call(
        put_beside,
        out_shape=jax.ShapeDtypeStruct((up.shape[0], up.shape[1] + down.size // up.shape[0]), LOW),
    )(up, down)


def per_device(
    sizes,
    tokens,
    w_qkv,
    w_out,
    w_up,
    w_down,
    norm1_scale,
    norm1_offset,
    qv_bias,
    out_bias,
    norm2_scale,
    norm2_offset,
    up_bias,
    down_bias,
    cotangent,
    counts,
):
    devices = sizes["fsdp"] * sizes["dp"]
    images, seq_len, width = tokens.shape
    share = width // devices
    rows = -(-seq_len // 16) * 16
    row_count = images * rows
    factor = (width // HEADS) ** -0.5
    small = (norm1_scale, norm1_offset, qv_bias, out_bias, norm2_scale, norm2_offset, up_bias, down_bias)
    small_sizes = [v.shape[0] for v in small]

    side = -(-sum(small_sizes) // 128)

    def small_split(flat):
        at, parts = 0, []
        for size in small_sizes:
            parts.append(flat[:, at : at + size])
            at += size
        return parts

    def small_join(parts):
        total, at = 0, 0
        for part in parts:
            size = part.shape[-1]
            ends = [(0, 0)] * (part.ndim - 1) + [(at, side * 128 - at - size)]
            total = total + jnp.pad(part, ends)
            at += size
        return total

    hidden_width = w_up.shape[1]
    ratio = hidden_width // width
    whole = lax.all_gather(beside(w_up, w_down), AXES, axis=0, tiled=True)
    small_block = jnp.pad(small_join(small).reshape(side, 128), ((0, share - side), (0, 0)))
    first = jnp.concatenate([w_qkv, w_out, small_block], axis=1)
    left, right = gathered(first, 2 * width, sizes)
    full_qkv = jnp.concatenate([left, right[:, :width]], axis=1)
    full_out = right[:, width : 2 * width]
    small_whole = right[:, 2 * width :].reshape(devices, share, 128)[:, :side].reshape(devices, -1)
    vectors = laid_out(small_whole, small_sizes)
    scale_one, offset_one, qv_full, out_shift, scale_two, offset_two, up_shift, down_shift = vectors
    full_up = whole[:, :hidden_width]
    full_down = [whole[:, to : to + width].reshape(devices, share, width) for to in range(hidden_width, 2 * hidden_width, width)]
    full_down = jnp.stack(full_down, axis=1).reshape(hidden_width, width)

    def padded(array):
        return jnp.pad(array, ((0, 0), (0, rows - seq_len), (0, 0))).reshape(row_count, width)

    live = (jnp.arange(images) < counts[0])[:, None, None]
    inputs = padded(tokens).astype(WIDE)
    seed_low = padded(jnp.where(live, cotangent, jnp.zeros((), LOW)))

    normed = (centred(inputs)[0] * scale_one + offset_one).astype(LOW)
    bias_full = jnp.concatenate([qv_full[:, :width], jnp.zeros((1, width), WIDE), qv_full[:, width:]], axis=1)
    projected = (dot(normed, full_qkv) + bias_full).astype(LOW).reshape(images, rows, 3 * width)
    head_out = attention(projected, seq_len, factor).reshape(row_count, width)
    middle = inputs + dot(head_out, full_out) + out_shift
    normed_two = (centred(middle)[0] * scale_two + offset_two).astype(LOW)
    active, slope = expanded(normed_two, whole, up_shift, rows)
    result = (middle + dot(active, full_down) + down_shift).reshape(images, rows, width)[:, :seq_len]
    out_tokens = jnp.where(live, result, 0.0).astype(LOW)

    grad_down = dot(active, seed_low, TN).astype(LOW)
    seed_again, grad_down = lax.optimization_barrier((seed_low, grad_down))
    down_sum = lax.psum_scatter(grad_down, AXES, scatter_dimension=0, tiled=True)
    back_hidden = (dot(seed_again, full_down, NT) * slope.astype(WIDE)).astype(LOW)
    grad_up = dot(normed_two, back_hidden, TN).astype(LOW)
    back_hidden, grad_up = lax.optimization_barrier((back_hidden, grad_up))
    up_sums = [Scatter([grad_up[:, : hidden_width // 2]], 0, sizes), Scatter([grad_up[:, hidden_width // 2 :]], 1, sizes)]

    def step(value):
        for part in up_sums:
            value = part.step_and_tie(value)
        return value

    back_two = step(dot(back_hidden, full_up, NT))
    middle_part, grad_scale_two, grad_offset_two = norm_back(middle, scale_two, back_two)
    back_middle = seed_low.astype(WIDE) + middle_part
    back_branch = back_middle.astype(LOW)
    grad_out = dot(head_out, back_branch, TN).astype(LOW)
    back_head = dot(back_branch, full_out, NT).astype(LOW).reshape(images, rows, width)
    back_projected = attention_back(projected, back_head, seq_len, factor, 2, {2: step, 4: step})
    back_projected = back_projected.reshape(row_count, 3 * width)
    grad_qkv = step(dot(normed, back_projected, TN).astype(LOW))
    back_projected, grad_qkv = lax.optimization_barrier((back_projected, grad_qkv))
    back_one = step(dot(back_projected, full_qkv, NT))
    input_part, grad_scale_one, grad_offset_one = norm_back(inputs, scale_one, back_one)
    grad_inputs = (back_middle + input_part).reshape(images, rows, width)[:, :seq_len]
    sums = column_total(back_projected)
    small_grads = (
        grad_scale_one,
        grad_offset_one,
        jnp.concatenate([sums[:width], sums[2 * width :]]),
        column_total(back_branch),
        grad_scale_two,
        grad_offset_two,
        column_total(back_hidden),
        column_total(seed_low),
    )
    small_block = small_join([v.reshape(devices, -1) for v in small_grads]).astype(LOW).reshape(devices, side, 128)
    small_block = jnp.pad(small_block, ((0, 0), (0, share - side), (0, 0))).reshape(width, 128)
    small_block, down_sum = lax.optimization_barrier((small_block, down_sum))
    late_one = Scatter([grad_qkv[:, : 2 * width]], 0, sizes).result()
    late_two = Scatter([grad_qkv[:, 2 * width :], grad_out, small_block], 1, sizes).result()
    small_out = [v[0] for v in small_split(late_two[:side, 2 * width :].reshape(1, -1))]
    return (
        out_tokens,
        grad_inputs,
        jnp.concatenate([late_one, late_two[:, :width]], axis=1),
        late_two[:, width : 2 * width],
        jnp.concatenate([part.result() for part in up_sums], axis=1),
        down_sum.astype(WIDE),
        *small_out,
    )


def solution(mesh):
    split = P(AXES)
    return jax.shard_map(
        functools.partial(per_device, dict(mesh.shape)),
        mesh=mesh,
        in_specs=(split,) * 15,
        out_specs=(split,) * 14,
        check_vma=False,
    )
```

```python
import functools
import math

import jax
import jax.numpy as jnp
from jax import lax
from jax.experimental import pallas as pl
from jax.experimental.pallas import tpu as pltpu
from jax.sharding import PartitionSpec as P

HEADS = 12
EPSILON = 1e-06
AXES = ("fsdp", "dp")
LOW = jnp.bfloat16
WIDE = jnp.float32
NN = (((1,), (0,)), ((), ()))
NT = (((1,), (1,)), ((), ()))
TN = (((0,), (0,)), ((), ()))


def dot(a, b, dims=NN):
    return lax.dot_general(a, b, dims, preferred_element_type=WIDE)


def attend(seq_len, factor, proj_ref, out_ref):
    rows, model_width = out_ref.shape[1:]
    lane = lax.broadcasted_iota(jnp.int32, (1, 128), 1)
    key_at = lax.broadcasted_iota(jnp.int32, (1, rows), 1)
    ones = jnp.ones((rows, 128), jnp.bfloat16)
    zero = jnp.zeros((), jnp.bfloat16)
    for pair in range(model_width // 128):
        at = pair * 128
        queries = proj_ref[0, :, at : at + 128]
        keys = proj_ref[0, :, model_width + at : model_width + at + 128]
        values = proj_ref[0, :, 2 * model_width + at : 2 * model_width + at + 128]
        wide = jnp.concatenate([values, ones], axis=1)
        halves = []
        for half in range(2):
            mine = (lane < 64) if half == 0 else (lane >= 64)
            scores = dot(jnp.where(mine, queries, zero), keys, NT)
            scores = jnp.where(key_at < seq_len, scores, -jnp.inf)
            top = jnp.max(scores, axis=1, keepdims=True)
            expo = jnp.exp2((scores - top) * (factor * math.log2(math.e))).astype(jnp.bfloat16)
            both = dot(expo, wide, NN)
            halves.append(both[:, :128] / both[:, 128:])
        out_ref[0, :, at : at + 128] = jnp.where(lane < 64, halves[0], halves[1]).astype(jnp.bfloat16)


def attend_back(seq_len, factor, proj_ref, back_ref, *refs):
    out_ref = refs[-1]
    rows, model_width = back_ref.shape[1:]
    lane = lax.broadcasted_iota(jnp.int32, (1, 128), 1)
    key_at = lax.broadcasted_iota(jnp.int32, (rows, 1), 0)
    zero = jnp.zeros((), jnp.bfloat16)
    for pair in range(model_width // 128):
        at = pair * 128
        queries = proj_ref[0, :, at : at + 128]
        keys = proj_ref[0, :, model_width + at : model_width + at + 128]
        values = proj_ref[0, :, 2 * model_width + at : 2 * model_width + at + 128]
        back = back_ref[0, :, at : at + 128]
        sides = (lane < 64, lane >= 64)
        queries_one = [jnp.where(mine, queries, zero) for mine in sides]
        back_one = [jnp.where(mine, back, zero) for mine in sides]
        scaled, probs_low = [], []
        for half in range(2):
            scores = dot(keys, queries_one[half], NT)
            back_probs = dot(values, back_one[half], NT)
            scores = jnp.where(key_at < seq_len, scores, -jnp.inf)
            top = jnp.max(scores, axis=0, keepdims=True)
            expo = jnp.exp2((scores - top) * (factor * math.log2(math.e)))
            probs = expo * (1.0 / jnp.sum(expo, axis=0, keepdims=True))
            row_dot = jnp.sum(probs * back_probs, axis=0, keepdims=True)
            scaled.append((probs * ((back_probs - row_dot) * factor)).astype(jnp.bfloat16))
            probs_low.append(probs.astype(jnp.bfloat16))
        back_queries = jnp.where(lane < 64, dot(scaled[0], keys, TN), dot(scaled[1], keys, TN))
        back_keys = dot(scaled[0], queries_one[0]) + dot(scaled[1], queries_one[1])
        back_values = dot(probs_low[0], back_one[0]) + dot(probs_low[1], back_one[1])
        for block, to in ((back_queries, 0), (back_keys, model_width), (back_values, 2 * model_width)):
            out_ref[0, :, to + at : to + at + 128] = block.astype(jnp.bfloat16)


def whole(shape):
    return pl.BlockSpec((1,) + shape, lambda i: (i, 0, 0))


def attention(projected, seq_len, factor):
    images, rows, wide = projected.shape
    return pl.pallas_call(
        functools.partial(attend, seq_len, factor),
        grid=(images,),
        in_specs=[whole((rows, wide))],
        out_specs=whole((rows, wide // 3)),
        out_shape=jax.ShapeDtypeStruct((images, rows, wide // 3), jnp.bfloat16),
        compiler_params=pltpu.CompilerParams(vmem_limit_bytes=40 << 20),
    )(projected)


def attention_back(projected, back_head, seq_len, factor, group, ties):
    images, rows, wide = projected.shape
    done = None
    for start in range(0, images, group):
        def block(shape, start=start):
            return pl.BlockSpec((1,) + shape, lambda i: (i + start, 0, 0))

        if ties.get(start):
            back_head = ties[start](back_head)
        kept = () if done is None else (done,)
        done = pl.pallas_call(
            functools.partial(attend_back, seq_len, factor),
            grid=(min(group, images - start),),
            in_specs=[block((rows, wide)), block((rows, wide // 3))] + [pl.BlockSpec(memory_space=pl.ANY)] * len(kept),
            out_specs=block((rows, wide)),
            out_shape=jax.ShapeDtypeStruct((images, rows, wide), jnp.bfloat16),
            input_output_aliases={2: 0} if kept else {},
            compiler_params=pltpu.CompilerParams(vmem_limit_bytes=40 << 20),
            cost_estimate=pl.CostEstimate(
                flops=group * HEADS * 10 * rows * rows * 256, bytes_accessed=14 * group * rows * wide, transcendentals=0
            ),
        )(projected, back_head, *kept)
    return done


def gelu_and_slope(hidden):
    below = 0.5 + 0.5 * lax.erf(hidden * math.sqrt(0.5))
    bell = jnp.exp2(hidden * hidden * (-0.5 * math.log2(math.e)))
    return hidden * below, below + hidden * bell * (1.0 / math.sqrt(2.0 * math.pi))


def expand(step, rows_ref, weight_ref, shift_ref, active_ref, slope_ref):
    for start in range(0, rows_ref.shape[0], step):
        at = pl.ds(start, step)
        hidden = dot(rows_ref[at, :], weight_ref[...]) + shift_ref[...]
        active, slope = gelu_and_slope(hidden)
        active_ref[at, :] = active.astype(LOW)
        slope_ref[at, :] = slope.astype(LOW)


def expanded(rows, weight, shift, step, width=512):
    count, depth = rows.shape
    full = shift.shape[1]
    out = jax.ShapeDtypeStruct((count, full), LOW)
    spec = pl.BlockSpec((count, width), lambda j: (0, j))
    return pl.pallas_call(
        functools.partial(expand, step),
        grid=(full // width,),
        in_specs=[
            pl.BlockSpec((count, depth), lambda j: (0, 0)),
            pl.BlockSpec((depth, width), lambda j: (0, j)),
            pl.BlockSpec((1, width), lambda j: (0, j)),
        ],
        out_specs=[spec, spec],
        out_shape=[out, out],
        compiler_params=pltpu.CompilerParams(vmem_limit_bytes=40 << 20),
        cost_estimate=pl.CostEstimate(
            flops=2 * count * depth * full, bytes_accessed=6 * count * full, transcendentals=2 * count * full
        ),
    )(rows, weight, shift)


def centred(values):
    center = values - jnp.mean(values, axis=-1, keepdims=True)
    rate = lax.rsqrt(jnp.mean(center * center, axis=-1, keepdims=True) + EPSILON)
    return center * rate, rate


def norm_back(values, scale, grad):
    unit, rate = centred(values)
    scaled = grad * scale
    inner = jnp.mean(scaled * unit, axis=-1, keepdims=True)
    back = rate * (scaled - jnp.mean(scaled, axis=-1, keepdims=True) - unit * inner)
    return back, jnp.sum(grad * unit, axis=0, keepdims=True), jnp.sum(grad, axis=0, keepdims=True)


def column_total(values):
    return jnp.sum(values.astype(WIDE), axis=0, keepdims=True)


def places(sizes):
    return [(name, 1 << k) for name in AXES for k in reversed(range(sizes[name].bit_length() - 1))]


def flipped(block, name, bit, sizes):
    return lax.ppermute(block, name, [(i, i ^ bit) for i in range(sizes[name])])


def is_set(name, bit):
    return (lax.axis_index(name) & bit) != 0


def routes(sizes):
    order = places(sizes)
    far = [p for p in order if p[0] == "fsdp" and p[1] > 1]
    near = [p for p in order if p[0] == "fsdp" and p[1] == 1]
    other = [p for p in order if p[0] == "dp" and p[1] > 1]
    core = [p for p in order if p[0] == "dp" and p[1] == 1]
    return far, near + other, other + near, core


def gather_by(block, steps, done, order, sizes):
    for place in steps:
        got = flipped(block, *place, sizes)
        high = is_set(*place)
        at = sum(order.index(p) < order.index(place) for p in done)
        block = jnp.stack([jnp.where(high, got, block), jnp.where(high, block, got)], axis=at)
        done = done + [place]
    return block, done


def gathered(block, half, sizes):
    order = places(sizes)
    far, one_way, other_way, core = routes(sizes)
    block, done = gather_by(block, far, [], order, sizes)
    parts = []
    for part, way in ((block[..., :half], one_way), (block[..., half:], other_way)):
        part, _ = gather_by(part, way + core, done, order, sizes)
        parts.append(part.reshape(-1, part.shape[-1]))
    return parts


def halved(block, place, left, sizes, kind=LOW):
    at = left.index(place)
    bit = is_set(*place).astype(jnp.int32)
    got = flipped(lax.dynamic_index_in_dim(block, 1 - bit, at, keepdims=False), *place, sizes)
    mine = lax.dynamic_index_in_dim(block, bit, at, keepdims=False)
    return (mine.astype(WIDE) + got.astype(WIDE)).astype(kind)


class Scatter:
    def __init__(self, arrays, way, sizes):
        far, one_way, other_way, core = routes(sizes)
        self.sizes = sizes
        self.left = places(sizes)
        self.plan = core + (one_way, other_way)[way][::-1] + far[::-1]
        self.block = None
        place = self.plan[0]
        bit = is_set(*place).astype(jnp.int32)
        cut = [a.reshape((-1, 2, a.shape[0] >> len(self.left), a.shape[1])) for a in arrays]

        def half_of(at):
            return jnp.concatenate([lax.dynamic_index_in_dim(a, at, 1, keepdims=False) for a in cut], axis=-1)

        self.theirs = half_of(1 - bit)
        self.mine = half_of(bit)

    def step(self):
        if not self.plan:
            return
        place, self.plan = self.plan[0], self.plan[1:]
        if self.block is None:
            got = flipped(self.theirs, *place, self.sizes)
            block = (self.mine.astype(WIDE) + got.astype(WIDE)).astype(LOW)
            self.block = block.reshape((2,) * (len(self.left) - 1) + block.shape[1:])
        else:
            self.block = halved(self.block, place, self.left, self.sizes, LOW if self.plan else WIDE)
        self.left = [q for q in self.left if q != place]

    def step_and_tie(self, value):
        self.step()
        value, self.block = lax.optimization_barrier((value, self.block))
        return value

    def cut_and_tie(self, value):
        value, self.theirs = lax.optimization_barrier((value, self.theirs))
        return value

    def result(self):
        while self.plan:
            self.step()
        return self.block


def scattered_small(blocks, sizes):
    left = places(sizes)
    blocks = blocks.reshape((2,) * len(left) + blocks.shape[1:])
    while left:
        blocks = halved(blocks, left[-1], left, sizes, WIDE)
        left = left[:-1]
    return blocks


def lay_out(sizes_of, block_ref, out_ref):
    devices = block_ref.shape[0]
    shares = block_ref[...].astype(WIDE)
    at, to = 0, 0
    for size in sizes_of:
        full = devices * size
        row = lax.broadcasted_iota(jnp.int32, (block_ref.shape[1], full), 0)
        column = lax.broadcasted_iota(jnp.int32, (block_ref.shape[1], full), 1)
        pick = jnp.where(row == at + lax.rem(column, size), 1.0, 0.0).astype(LOW)
        spread = dot(shares.astype(LOW), pick)
        device = lax.broadcasted_iota(jnp.int32, (devices, full), 0)
        own = lax.div(lax.broadcasted_iota(jnp.int32, (devices, full), 1), size)
        out_ref[:, to : to + full] = jnp.sum(jnp.where(device == own, spread, 0.0), axis=0, keepdims=True)
        at += size
        to += full


def laid_out(block, sizes_of):
    full = block.shape[0] * sum(sizes_of)
    flat = pl.pallas_call(
        functools.partial(lay_out, sizes_of),
        out_shape=jax.ShapeDtypeStruct((1, full), WIDE),
        compiler_params=pltpu.CompilerParams(vmem_limit_bytes=40 << 20),
    )(block)
    parts, at = [], 0
    for size in sizes_of:
        parts.append(flat[:, at : at + block.shape[0] * size])
        at += block.shape[0] * size
    return parts


def share_out(vector_count, *refs):
    out_ref = refs[vector_count]
    devices = out_ref.shape[0]
    for i, ref in enumerate(refs[:vector_count]):
        full = ref.shape[1]
        size = full // devices
        device = lax.broadcasted_iota(jnp.int32, (devices, full), 0)
        own = lax.div(lax.broadcasted_iota(jnp.int32, (devices, full), 1), size)
        pick = lax.rem(lax.broadcasted_iota(jnp.int32, (full, 128), 0), size)
        pick = jnp.where(pick == lax.broadcasted_iota(jnp.int32, (full, 128), 1), 1.0, 0.0).astype(LOW)
        spread = jnp.where(device == own, ref[...], 0.0)
        high = spread.astype(LOW)
        rest = (spread - high.astype(WIDE)).astype(LOW)
        out_ref[:, i * 128 : (i + 1) * 128] = dot(high, pick) + dot(rest, pick)


def shared_out(vectors, devices):
    return pl.pallas_call(
        functools.partial(share_out, len(vectors)),
        out_shape=jax.ShapeDtypeStruct((devices, 128 * len(vectors)), WIDE),
        compiler_params=pltpu.CompilerParams(vmem_limit_bytes=40 << 20),
    )(*vectors)


def put_beside(up_ref, down_ref, out_ref):
    share, hidden_width = up_ref.shape
    width = down_ref.shape[1]
    out_ref[:, :hidden_width] = up_ref[...]
    down = down_ref[...].astype(WIDE)
    for i in range(down.shape[0] // share):
        to = hidden_width + i * width
        out_ref[:, to : to + width] = down[i * share : (i + 1) * share].astype(LOW)


def beside(up, down):
    return pl.pallas_call(
        put_beside,
        out_shape=jax.ShapeDtypeStruct((up.shape[0], up.shape[1] + down.size // up.shape[0]), LOW),
    )(up, down)


def per_device(
    sizes,
    tokens,
    w_qkv,
    w_out,
    w_up,
    w_down,
    norm1_scale,
    norm1_offset,
    qv_bias,
    out_bias,
    norm2_scale,
    norm2_offset,
    up_bias,
    down_bias,
    cotangent,
    counts,
):
    devices = sizes["fsdp"] * sizes["dp"]
    images, seq_len, width = tokens.shape
    share = width // devices
    rows = -(-seq_len // 16) * 16
    row_count = images * rows
    factor = (width // HEADS) ** -0.5
    small = (norm1_scale, norm1_offset, qv_bias, out_bias, norm2_scale, norm2_offset, up_bias, down_bias)
    small_sizes = [v.shape[0] for v in small]

    side = -(-sum(small_sizes) // 128)

    def small_split(flat):
        at, parts = 0, []
        for size in small_sizes:
            parts.append(flat[:, at : at + size])
            at += size
        return parts

    def small_join(parts):
        total, at = 0, 0
        for part in parts:
            size = part.shape[-1]
            ends = [(0, 0)] * (part.ndim - 1) + [(at, side * 128 - at - size)]
            total = total + jnp.pad(part, ends)
            at += size
        return total

    hidden_width = w_up.shape[1]
    ratio = hidden_width // width
    whole = lax.all_gather(beside(w_up, w_down), AXES, axis=0, tiled=True)
    small_block = jnp.pad(small_join(small).reshape(side, 128), ((0, share - side), (0, 0)))
    first = jnp.concatenate([w_qkv, w_out, small_block], axis=1)
    left, right = gathered(first, 2 * width, sizes)
    full_qkv = jnp.concatenate([left, right[:, :width]], axis=1)
    full_out = right[:, width : 2 * width]
    small_whole = right[:, 2 * width :].reshape(devices, share, 128)[:, :side].reshape(devices, -1)
    vectors = laid_out(small_whole, small_sizes)
    scale_one, offset_one, qv_full, out_shift, scale_two, offset_two, up_shift, down_shift = vectors
    full_up = whole[:, :hidden_width]
    full_down = [whole[:, to : to + width].reshape(devices, share, width) for to in range(hidden_width, 2 * hidden_width, width)]
    full_down = jnp.stack(full_down, axis=1).reshape(hidden_width, width)

    def padded(array):
        return jnp.pad(array, ((0, 0), (0, rows - seq_len), (0, 0))).reshape(row_count, width)

    live = (jnp.arange(images) < counts[0])[:, None, None]
    inputs = padded(tokens).astype(WIDE)
    seed_low = padded(jnp.where(live, cotangent, jnp.zeros((), LOW)))

    normed = (centred(inputs)[0] * scale_one + offset_one).astype(LOW)
    bias_full = jnp.concatenate([qv_full[:, :width], jnp.zeros((1, width), WIDE), qv_full[:, width:]], axis=1)
    projected = (dot(normed, full_qkv) + bias_full).astype(LOW).reshape(images, rows, 3 * width)
    head_out = attention(projected, seq_len, factor).reshape(row_count, width)
    middle = inputs + dot(head_out, full_out) + out_shift
    normed_two = (centred(middle)[0] * scale_two + offset_two).astype(LOW)
    active, slope = expanded(normed_two, whole, up_shift, rows)
    grad_down = dot(active, seed_low, TN).astype(LOW)
    seed_again, grad_down = lax.optimization_barrier((seed_low, grad_down))
    down_sum = lax.psum_scatter(grad_down, AXES, scatter_dimension=0, tiled=True)
    back_hidden = (dot(seed_again, full_down, NT) * slope.astype(WIDE)).astype(LOW)
    grad_up = dot(normed_two, back_hidden, TN).astype(LOW)
    back_hidden, grad_up = lax.optimization_barrier((back_hidden, grad_up))
    up_sums = [Scatter([grad_up[:, : hidden_width // 2]], 0, sizes), Scatter([grad_up[:, hidden_width // 2 :]], 1, sizes)]

    def step(value):
        for part in up_sums:
            value = part.step_and_tie(value)
        return value

    back_two = step(dot(back_hidden, full_up, NT))
    middle_part, grad_scale_two, grad_offset_two = norm_back(middle, scale_two, back_two)
    back_middle = seed_low.astype(WIDE) + middle_part
    back_branch = back_middle.astype(LOW)
    grad_out = dot(head_out, back_branch, TN).astype(LOW)
    back_head = dot(back_branch, full_out, NT).astype(LOW).reshape(images, rows, width)
    back_projected = attention_back(projected, back_head, seq_len, factor, 2, {2: step, 4: step})
    back_projected = back_projected.reshape(row_count, 3 * width)
    grad_qkv = step(dot(normed, back_projected, TN).astype(LOW))
    back_projected, grad_qkv = lax.optimization_barrier((back_projected, grad_qkv))
    late = [
        Scatter([grad_qkv[:, : 2 * width]], 0, sizes),
        Scatter([grad_qkv[:, 2 * width :], grad_out], 1, sizes),
    ]
    for part in late:
        back_projected = part.cut_and_tie(back_projected)
    back_one = step(dot(back_projected, full_qkv, NT))
    for part in late:
        back_one = part.step_and_tie(back_one)
    input_part, grad_scale_one, grad_offset_one = norm_back(inputs, scale_one, back_one)
    grad_inputs = (back_middle + input_part).reshape(images, rows, width)[:, :seq_len]
    active, late[0].block = lax.optimization_barrier((active, late[0].block))
    result = (middle + dot(active, full_down) + down_shift).reshape(images, rows, width)[:, :seq_len]
    out_tokens = jnp.where(live, result, 0.0).astype(LOW)
    sums = column_total(back_projected)
    small_grads = (
        grad_scale_one,
        grad_offset_one,
        jnp.concatenate([sums[:, :width], sums[:, 2 * width :]], axis=1),
        column_total(back_branch),
        grad_scale_two,
        grad_offset_two,
        column_total(back_hidden),
        column_total(seed_low),
    )
    small_block, down_sum = lax.optimization_barrier((shared_out(small_grads, devices), down_sum))
    small_sum = scattered_small(small_block, sizes)
    small_out = [small_sum[i * 128 : i * 128 + size] for i, size in enumerate(small_sizes)]
    late_one, late_two = [part.result() for part in late]
    return (
        out_tokens,
        grad_inputs,
        jnp.concatenate([late_one, late_two[:, :width]], axis=1),
        late_two[:, width:],
        jnp.concatenate([part.result() for part in up_sums], axis=1),
        down_sum.astype(WIDE),
        *small_out,
    )


def solution(mesh):
    split = P(AXES)
    return jax.shard_map(
        functools.partial(per_device, dict(mesh.shape)),
        mesh=mesh,
        in_specs=(split,) * 15,
        out_specs=(split,) * 14,
        check_vma=False,
    )
```

```python
import functools
import math

import jax
import jax.numpy as jnp
from jax import lax
from jax.experimental import pallas as pl
from jax.experimental.pallas import tpu as pltpu
from jax.sharding import PartitionSpec as P

HEADS = 12
EPSILON = 1e-06
AXES = ("fsdp", "dp")
LOW = jnp.bfloat16
WIDE = jnp.float32
NN = (((1,), (0,)), ((), ()))
NT = (((1,), (1,)), ((), ()))
TN = (((0,), (0,)), ((), ()))


def dot(a, b, dims=NN):
    return lax.dot_general(a, b, dims, preferred_element_type=WIDE)


def attend(seq_len, factor, proj_ref, out_ref):
    rows, model_width = out_ref.shape[1:]
    lane = lax.broadcasted_iota(jnp.int32, (1, 128), 1)
    key_at = lax.broadcasted_iota(jnp.int32, (1, rows), 1)
    ones = jnp.ones((rows, 128), jnp.bfloat16)
    zero = jnp.zeros((), jnp.bfloat16)
    for pair in range(model_width // 128):
        at = pair * 128
        queries = proj_ref[0, :, at : at + 128]
        keys = proj_ref[0, :, model_width + at : model_width + at + 128]
        values = proj_ref[0, :, 2 * model_width + at : 2 * model_width + at + 128]
        wide = jnp.concatenate([values, ones], axis=1)
        halves = []
        for half in range(2):
            mine = (lane < 64) if half == 0 else (lane >= 64)
            scores = dot(jnp.where(mine, queries, zero), keys, NT)
            scores = jnp.where(key_at < seq_len, scores, -jnp.inf)
            top = jnp.max(scores, axis=1, keepdims=True)
            expo = jnp.exp2((scores - top) * (factor * math.log2(math.e))).astype(jnp.bfloat16)
            both = dot(expo, wide, NN)
            halves.append(both[:, :128] / both[:, 128:])
        out_ref[0, :, at : at + 128] = jnp.where(lane < 64, halves[0], halves[1]).astype(jnp.bfloat16)


def attend_back(seq_len, factor, proj_ref, back_ref, *refs):
    out_ref = refs[-1]
    rows, model_width = back_ref.shape[1:]
    lane = lax.broadcasted_iota(jnp.int32, (1, 128), 1)
    key_at = lax.broadcasted_iota(jnp.int32, (rows, 1), 0)
    zero = jnp.zeros((), jnp.bfloat16)
    for pair in range(model_width // 128):
        at = pair * 128
        queries = proj_ref[0, :, at : at + 128]
        keys = proj_ref[0, :, model_width + at : model_width + at + 128]
        values = proj_ref[0, :, 2 * model_width + at : 2 * model_width + at + 128]
        back = back_ref[0, :, at : at + 128]
        sides = (lane < 64, lane >= 64)
        queries_one = [jnp.where(mine, queries, zero) for mine in sides]
        back_one = [jnp.where(mine, back, zero) for mine in sides]
        scaled, probs_low = [], []
        for half in range(2):
            scores = dot(keys, queries_one[half], NT)
            back_probs = dot(values, back_one[half], NT)
            scores = jnp.where(key_at < seq_len, scores, -jnp.inf)
            top = jnp.max(scores, axis=0, keepdims=True)
            expo = jnp.exp2((scores - top) * (factor * math.log2(math.e)))
            probs = expo * (1.0 / jnp.sum(expo, axis=0, keepdims=True))
            row_dot = jnp.sum(probs * back_probs, axis=0, keepdims=True)
            scaled.append((probs * ((back_probs - row_dot) * factor)).astype(jnp.bfloat16))
            probs_low.append(probs.astype(jnp.bfloat16))
        back_queries = jnp.where(lane < 64, dot(scaled[0], keys, TN), dot(scaled[1], keys, TN))
        back_keys = dot(scaled[0], queries_one[0]) + dot(scaled[1], queries_one[1])
        back_values = dot(probs_low[0], back_one[0]) + dot(probs_low[1], back_one[1])
        for block, to in ((back_queries, 0), (back_keys, model_width), (back_values, 2 * model_width)):
            out_ref[0, :, to + at : to + at + 128] = block.astype(jnp.bfloat16)


def whole(shape):
    return pl.BlockSpec((1,) + shape, lambda i: (i, 0, 0))


def attention(projected, seq_len, factor):
    images, rows, wide = projected.shape
    return pl.pallas_call(
        functools.partial(attend, seq_len, factor),
        grid=(images,),
        in_specs=[whole((rows, wide))],
        out_specs=whole((rows, wide // 3)),
        out_shape=jax.ShapeDtypeStruct((images, rows, wide // 3), jnp.bfloat16),
        compiler_params=pltpu.CompilerParams(vmem_limit_bytes=40 << 20),
    )(projected)


def attention_back(projected, back_head, seq_len, factor, group, ties):
    images, rows, wide = projected.shape
    done = None
    for start in range(0, images, group):
        def block(shape, start=start):
            return pl.BlockSpec((1,) + shape, lambda i: (i + start, 0, 0))

        if ties.get(start):
            back_head = ties[start](back_head)
        kept = () if done is None else (done,)
        done = pl.pallas_call(
            functools.partial(attend_back, seq_len, factor),
            grid=(min(group, images - start),),
            in_specs=[block((rows, wide)), block((rows, wide // 3))] + [pl.BlockSpec(memory_space=pl.ANY)] * len(kept),
            out_specs=block((rows, wide)),
            out_shape=jax.ShapeDtypeStruct((images, rows, wide), jnp.bfloat16),
            input_output_aliases={2: 0} if kept else {},
            compiler_params=pltpu.CompilerParams(vmem_limit_bytes=40 << 20),
            cost_estimate=pl.CostEstimate(
                flops=group * HEADS * 10 * rows * rows * 256, bytes_accessed=14 * group * rows * wide, transcendentals=0
            ),
        )(projected, back_head, *kept)
    return done


def gelu_and_slope(hidden):
    below = 0.5 + 0.5 * lax.erf(hidden * math.sqrt(0.5))
    bell = jnp.exp2(hidden * hidden * (-0.5 * math.log2(math.e)))
    return hidden * below, below + hidden * bell * (1.0 / math.sqrt(2.0 * math.pi))


def expand(step, rows_ref, weight_ref, shift_ref, active_ref, slope_ref):
    for start in range(0, rows_ref.shape[0], step):
        at = pl.ds(start, step)
        hidden = dot(rows_ref[at, :], weight_ref[...]) + shift_ref[...]
        active, slope = gelu_and_slope(hidden)
        active_ref[at, :] = active.astype(LOW)
        slope_ref[at, :] = slope.astype(LOW)


def expanded(rows, weight, shift, step, width=512):
    count, depth = rows.shape
    full = shift.shape[1]
    out = jax.ShapeDtypeStruct((count, full), LOW)
    spec = pl.BlockSpec((count, width), lambda j: (0, j))
    return pl.pallas_call(
        functools.partial(expand, step),
        grid=(full // width,),
        in_specs=[
            pl.BlockSpec((count, depth), lambda j: (0, 0)),
            pl.BlockSpec((depth, width), lambda j: (0, j)),
            pl.BlockSpec((1, width), lambda j: (0, j)),
        ],
        out_specs=[spec, spec],
        out_shape=[out, out],
        compiler_params=pltpu.CompilerParams(vmem_limit_bytes=40 << 20),
        cost_estimate=pl.CostEstimate(
            flops=2 * count * depth * full, bytes_accessed=6 * count * full, transcendentals=2 * count * full
        ),
    )(rows, weight, shift)


def centred(values):
    center = values - jnp.mean(values, axis=-1, keepdims=True)
    rate = lax.rsqrt(jnp.mean(center * center, axis=-1, keepdims=True) + EPSILON)
    return center * rate, rate


def norm_back(values, scale, grad):
    unit, rate = centred(values)
    scaled = grad * scale
    inner = jnp.mean(scaled * unit, axis=-1, keepdims=True)
    back = rate * (scaled - jnp.mean(scaled, axis=-1, keepdims=True) - unit * inner)
    return back, jnp.sum(grad * unit, axis=0, keepdims=True), jnp.sum(grad, axis=0, keepdims=True)


def column_total(values):
    return jnp.sum(values.astype(WIDE), axis=0, keepdims=True)


def places(sizes):
    return [(name, 1 << k) for name in AXES for k in reversed(range(sizes[name].bit_length() - 1))]


def flipped(block, name, bit, sizes):
    return lax.ppermute(block, name, [(i, i ^ bit) for i in range(sizes[name])])


def is_set(name, bit):
    return (lax.axis_index(name) & bit) != 0


def routes(sizes):
    order = places(sizes)
    far = [p for p in order if p[0] == "fsdp" and p[1] > 1]
    near = [p for p in order if p[0] == "fsdp" and p[1] == 1]
    other = [p for p in order if p[0] == "dp" and p[1] > 1]
    core = [p for p in order if p[0] == "dp" and p[1] == 1]
    return far, near + other, other + near, core


def gather_by(block, steps, done, order, sizes):
    for place in steps:
        got = flipped(block, *place, sizes)
        high = is_set(*place)
        at = sum(order.index(p) < order.index(place) for p in done)
        block = jnp.stack([jnp.where(high, got, block), jnp.where(high, block, got)], axis=at)
        done = done + [place]
    return block, done


def gathered(block, half, tie, sizes):
    order = places(sizes)
    far, one_way, other_way, core = routes(sizes)
    block, done = gather_by(block, far, [], order, sizes)
    block = tie(block)
    parts = []
    for part, way in ((block[..., :half], one_way), (block[..., half:], other_way)):
        part, _ = gather_by(part, way + core, done, order, sizes)
        parts.append(part.reshape(-1, part.shape[-1]))
    return parts


def halved(block, place, left, sizes, kind=LOW):
    at = left.index(place)
    bit = is_set(*place).astype(jnp.int32)
    got = flipped(lax.dynamic_index_in_dim(block, 1 - bit, at, keepdims=False), *place, sizes)
    mine = lax.dynamic_index_in_dim(block, bit, at, keepdims=False)
    return (mine.astype(WIDE) + got.astype(WIDE)).astype(kind)


class Scatter:
    def __init__(self, arrays, way, sizes):
        far, one_way, other_way, core = routes(sizes)
        self.sizes = sizes
        self.left = places(sizes)
        self.plan = core + (one_way, other_way)[way][::-1]
        self.block = None
        place = self.plan[0]
        bit = is_set(*place).astype(jnp.int32)
        cut = [a.reshape((-1, 2, a.shape[0] >> len(self.left), a.shape[1])) for a in arrays]

        def half_of(at):
            return jnp.concatenate([lax.dynamic_index_in_dim(a, at, 1, keepdims=False) for a in cut], axis=-1)

        self.theirs = half_of(1 - bit)
        self.mine = half_of(bit)

    def step(self):
        place, self.plan = self.plan[0], self.plan[1:]
        if self.block is None:
            got = flipped(self.theirs, *place, self.sizes)
            block = (self.mine.astype(WIDE) + got.astype(WIDE)).astype(LOW)
            self.block = block.reshape((2,) * (len(self.left) - 1) + block.shape[1:])
        else:
            self.block = halved(self.block, place, self.left, self.sizes)
        self.left = [q for q in self.left if q != place]

    def step_and_tie(self, value):
        self.step()
        value, self.block = lax.optimization_barrier((value, self.block))
        return value

    def cut_and_tie(self, value):
        value, self.theirs = lax.optimization_barrier((value, self.theirs))
        return value


class Far:
    def __init__(self, parts, sizes):
        for part in parts:
            while part.plan:
                part.step()
        self.sizes = sizes
        self.plan = routes(sizes)[0][::-1]
        self.left = parts[0].left
        self.block = jnp.concatenate([part.block for part in parts], axis=-1)

    def step(self):
        place, self.plan = self.plan[0], self.plan[1:]
        self.block = halved(self.block, place, self.left, self.sizes, LOW if self.plan else WIDE)
        self.left = [q for q in self.left if q != place]

    def result(self):
        while self.plan:
            self.step()
        return self.block


def together(parts):
    blocks = lax.optimization_barrier([part.block for part in parts])
    for part, block in zip(parts, blocks):
        part.block = block


def scattered_small(blocks, sizes):
    left = places(sizes)
    blocks = blocks.reshape((2,) * len(left) + blocks.shape[1:])
    while left:
        blocks = halved(blocks, left[-1], left, sizes, WIDE)
        left = left[:-1]
    return blocks


def lay_out(sizes_of, block_ref, out_ref):
    devices = block_ref.shape[0]
    shares = block_ref[...].astype(WIDE)
    at, to = 0, 0
    for size in sizes_of:
        full = devices * size
        row = lax.broadcasted_iota(jnp.int32, (block_ref.shape[1], full), 0)
        column = lax.broadcasted_iota(jnp.int32, (block_ref.shape[1], full), 1)
        pick = jnp.where(row == at + lax.rem(column, size), 1.0, 0.0).astype(LOW)
        spread = dot(shares.astype(LOW), pick)
        device = lax.broadcasted_iota(jnp.int32, (devices, full), 0)
        own = lax.div(lax.broadcasted_iota(jnp.int32, (devices, full), 1), size)
        out_ref[:, to : to + full] = jnp.sum(jnp.where(device == own, spread, 0.0), axis=0, keepdims=True)
        at += size
        to += full


def laid_out(block, sizes_of):
    full = block.shape[0] * sum(sizes_of)
    flat = pl.pallas_call(
        functools.partial(lay_out, sizes_of),
        out_shape=jax.ShapeDtypeStruct((1, full), WIDE),
        compiler_params=pltpu.CompilerParams(vmem_limit_bytes=40 << 20),
    )(block)
    parts, at = [], 0
    for size in sizes_of:
        parts.append(flat[:, at : at + block.shape[0] * size])
        at += block.shape[0] * size
    return parts


def share_out(vector_count, *refs):
    out_ref = refs[vector_count]
    devices = out_ref.shape[0]
    for i, ref in enumerate(refs[:vector_count]):
        full = ref.shape[1]
        size = full // devices
        device = lax.broadcasted_iota(jnp.int32, (devices, full), 0)
        own = lax.div(lax.broadcasted_iota(jnp.int32, (devices, full), 1), size)
        pick = lax.rem(lax.broadcasted_iota(jnp.int32, (full, 128), 0), size)
        pick = jnp.where(pick == lax.broadcasted_iota(jnp.int32, (full, 128), 1), 1.0, 0.0).astype(LOW)
        spread = jnp.where(device == own, ref[...], 0.0)
        high = spread.astype(LOW)
        rest = (spread - high.astype(WIDE)).astype(LOW)
        out_ref[:, i * 128 : (i + 1) * 128] = dot(high, pick) + dot(rest, pick)


def shared_out(vectors, devices):
    return pl.pallas_call(
        functools.partial(share_out, len(vectors)),
        out_shape=jax.ShapeDtypeStruct((devices, 128 * len(vectors)), WIDE),
        compiler_params=pltpu.CompilerParams(vmem_limit_bytes=40 << 20),
    )(*vectors)


def put_beside(up_ref, down_ref, out_ref):
    share, hidden_width = up_ref.shape
    width = down_ref.shape[1]
    out_ref[:, :hidden_width] = up_ref[...]
    down = down_ref[...].astype(WIDE)
    for i in range(down.shape[0] // share):
        to = hidden_width + i * width
        out_ref[:, to : to + width] = down[i * share : (i + 1) * share].astype(LOW)


def beside(up, down):
    return pl.pallas_call(
        put_beside,
        out_shape=jax.ShapeDtypeStruct((up.shape[0], up.shape[1] + down.size // up.shape[0]), LOW),
    )(up, down)


def per_device(
    sizes,
    tokens,
    w_qkv,
    w_out,
    w_up,
    w_down,
    norm1_scale,
    norm1_offset,
    qv_bias,
    out_bias,
    norm2_scale,
    norm2_offset,
    up_bias,
    down_bias,
    cotangent,
    counts,
):
    devices = sizes["fsdp"] * sizes["dp"]
    images, seq_len, width = tokens.shape
    share = width // devices
    rows = -(-seq_len // 16) * 16
    row_count = images * rows
    factor = (width // HEADS) ** -0.5
    small = (norm1_scale, norm1_offset, qv_bias, out_bias, norm2_scale, norm2_offset, up_bias, down_bias)
    small_sizes = [v.shape[0] for v in small]

    side = -(-sum(small_sizes) // 128)

    def small_split(flat):
        at, parts = 0, []
        for size in small_sizes:
            parts.append(flat[:, at : at + size])
            at += size
        return parts

    def small_join(parts):
        total, at = 0, 0
        for part in parts:
            size = part.shape[-1]
            ends = [(0, 0)] * (part.ndim - 1) + [(at, side * 128 - at - size)]
            total = total + jnp.pad(part, ends)
            at += size
        return total

    def padded(array):
        return jnp.pad(array, ((0, 0), (0, rows - seq_len), (0, 0))).reshape(row_count, width)

    live = (jnp.arange(images) < counts[0])[:, None, None]
    inputs = padded(tokens).astype(WIDE)

    early = {}

    def beside_gather(block):
        seed = padded(jnp.where(live, cotangent, jnp.zeros((), LOW)))
        block, early["seed"], early["total"] = lax.optimization_barrier((block, seed, column_total(seed)))
        return block

    hidden_width = w_up.shape[1]
    ratio = hidden_width // width
    whole = lax.all_gather(beside(w_up, w_down), AXES, axis=0, tiled=True)
    small_block = jnp.pad(small_join(small).reshape(side, 128), ((0, share - side), (0, 0)))
    first = jnp.concatenate([w_qkv, w_out, small_block], axis=1)
    left, right = gathered(first, 2 * width, beside_gather, sizes)
    seed_low = early["seed"]
    full_qkv = jnp.concatenate([left, right[:, :width]], axis=1)
    full_out = right[:, width : 2 * width]
    small_whole = right[:, 2 * width :].reshape(devices, share, 128)[:, :side].reshape(devices, -1)
    vectors = laid_out(small_whole, small_sizes)
    scale_one, offset_one, qv_full, out_shift, scale_two, offset_two, up_shift, down_shift = vectors
    full_up = whole[:, :hidden_width]
    full_down = [whole[:, to : to + width].reshape(devices, share, width) for to in range(hidden_width, 2 * hidden_width, width)]
    full_down = jnp.stack(full_down, axis=1).reshape(hidden_width, width)

    normed = (centred(inputs)[0] * scale_one + offset_one).astype(LOW)
    bias_full = jnp.concatenate([qv_full[:, :width], jnp.zeros((1, width), WIDE), qv_full[:, width:]], axis=1)
    projected = (dot(normed, full_qkv) + bias_full).astype(LOW).reshape(images, rows, 3 * width)
    head_out = attention(projected, seq_len, factor).reshape(row_count, width)
    middle = inputs + dot(head_out, full_out) + out_shift
    normed_two = (centred(middle)[0] * scale_two + offset_two).astype(LOW)
    active, slope = expanded(normed_two, whole, up_shift, rows)
    grad_down = dot(active, seed_low, TN).astype(LOW)
    seed_again, grad_down = lax.optimization_barrier((seed_low, grad_down))
    down_sum = lax.psum_scatter(grad_down, AXES, scatter_dimension=0, tiled=True)
    back_hidden = (dot(seed_again, full_down, NT) * slope.astype(WIDE)).astype(LOW)
    grad_up = dot(normed_two, back_hidden, TN).astype(LOW)
    back_hidden, grad_up = lax.optimization_barrier((back_hidden, grad_up))
    up_sums = [Scatter([grad_up[:, : hidden_width // 2]], 0, sizes), Scatter([grad_up[:, hidden_width // 2 :]], 1, sizes)]

    def step(value):
        for part in up_sums:
            value = part.step_and_tie(value)
        return value

    back_two = step(dot(back_hidden, full_up, NT))
    middle_part, grad_scale_two, grad_offset_two = norm_back(middle, scale_two, back_two)
    back_middle = seed_low.astype(WIDE) + middle_part
    back_branch = back_middle.astype(LOW)
    grad_out = dot(head_out, back_branch, TN).astype(LOW)
    back_head = dot(back_branch, full_out, NT).astype(LOW).reshape(images, rows, width)
    back_projected = attention_back(projected, back_head, seq_len, factor, 2, {2: step, 4: step})
    back_projected = back_projected.reshape(row_count, 3 * width)
    grad_qkv = dot(normed, back_projected, TN).astype(LOW)
    back_projected, grad_qkv = lax.optimization_barrier((back_projected, grad_qkv))
    late = [
        Scatter([grad_qkv[:, : 2 * width]], 0, sizes),
        Scatter([grad_qkv[:, 2 * width :], grad_out], 1, sizes),
    ]
    for part in late:
        back_projected = part.cut_and_tie(back_projected)
    back_one = dot(back_projected, full_qkv, NT)
    for part in late:
        back_one = part.step_and_tie(back_one)
    far_up = Far(up_sums, sizes)
    together([*late, far_up])
    input_part, grad_scale_one, grad_offset_one = norm_back(inputs, scale_one, back_one)
    grad_inputs = (back_middle + input_part).reshape(images, rows, width)[:, :seq_len]
    active, late[0].block = lax.optimization_barrier((active, late[0].block))
    result = (middle + dot(active, full_down) + down_shift).reshape(images, rows, width)[:, :seq_len]
    out_tokens = jnp.where(live, result, 0.0).astype(LOW)
    sums = column_total(back_projected)
    small_grads = (
        grad_scale_one,
        grad_offset_one,
        jnp.concatenate([sums[:, :width], sums[:, 2 * width :]], axis=1),
        column_total(back_branch),
        grad_scale_two,
        grad_offset_two,
        column_total(back_hidden),
        early["total"],
    )
    small_block, down_sum = lax.optimization_barrier((shared_out(small_grads, devices), down_sum))
    small_sum = scattered_small(small_block, sizes)
    small_out = [small_sum[i * 128 : i * 128 + size] for i, size in enumerate(small_sizes)]
    far_up.step()
    for part in late:
        part.step()
    together([*late, far_up])
    far_up.step()
    for part in late:
        part.step()
    far_late = Far(late, sizes)
    far_late.step()
    together([far_late, far_up])
    late_sum = far_late.result()
    return (
        out_tokens,
        grad_inputs,
        late_sum[:, : 3 * width],
        late_sum[:, 3 * width :],
        far_up.result(),
        down_sum.astype(WIDE),
        *small_out,
    )


def solution(mesh):
    split = P(AXES)
    return jax.shard_map(
        functools.partial(per_device, dict(mesh.shape)),
        mesh=mesh,
        in_specs=(split,) * 15,
        out_specs=(split,) * 14,
        check_vma=False,
    )
```
